256 devices in a mesh: gx: 16 (over y_hi, z), gy: 4 (over x), gz: 4 (over y_lo, core).
Axes of the slice: x: 4, y: 4 (y_hi: 2, y_lo: 2; y = y_hi * 2 + y_lo), z: 8, core: 2. Of those that a mesh axis runs over, the one named last changes fastest.
Arguments:
- features: bfloat16 [32, 8, 8, 32, 128], P('gx', 'gy', 'gz'), may hold values from -6 to 6
- positions: float32 [32, 8, 8, 3, 32], P('gx', 'gy', 'gz'), may hold values from 0 to 6, as said below
- counts: int32 [32, 8, 8], P('gx', 'gy', 'gz'), may hold values from 8 to 32, as said below
- species: int32 [32, 8, 8, 32], P('gx', 'gy', 'gz'), may hold values from 0 to 4
- radial_weight: float32 [8, 3, 128], replicated, may hold values from -0.21875 to 0.21875
- mix_weight: bfloat16 [128, 128], replicated, may hold values from -0.5 to 0.5
- skip_weight: bfloat16 [5, 128, 128], replicated, may hold values from -0.5 to 0.5
- readout: float32 [5, 128], replicated, may hold values from -3 to 3
Outputs:
- new_features: bfloat16 [32, 8, 8, 32, 128], P('gx', 'gy', 'gz')
- forces: float32 [32, 8, 8, 3, 32], P('gx', 'gy', 'gz')
- feature_grad: float32 [32, 8, 8, 32, 128], P('gx', 'gy', 'gz')
The draws below stay inside these ranges and needn't reach their ends.
Inputs may be any that keep to these rules, and one draw needn't show every extreme that they name: `counts`: some cell holds exactly 32 atoms. `positions`: coordinates lie inside the cell, atoms of one cell at least 0.6 angstroms apart.
All inputs are finite; a program needn't handle non-finite values.
Results may differ from the reference program's by a relative error of at most 0.023.
Values may be sent and summed in bfloat16 or wider, within the bound.
No kernel may reach another device: no remote copies, remote signals or barrier semaphores. Data moves between devices by JAX's collectives and lax.ppermute only.
A program may use at most 192 MiB of HBM per device.

```python
import math
from functools import partial
import jax
import jax.numpy as jnp
import numpy as np
from jax import lax

K = 128
NB = 8
SPECIES = 5
P_SIZE = 32
NX = 32
NY = 8
NZ = 8


def draw_positions(key, part):
    key = jax.random.fold_in(key, 11)
    slot_ids = jnp.arange(P_SIZE)
    layers = max(1, (P_SIZE + 15) // 16)
    spacing = jnp.array([1.5, 1.5, 6.0 / layers], jnp.float32)
    lattice = jnp.stack([slot_ids % 4, slot_ids // 4 % 4, slot_ids // 16]).astype(jnp.float32)
    centre = (lattice + 0.5) * spacing[:, None]
    noise = jax.random.uniform(key, (NX, NY, NZ, 3, P_SIZE), jnp.float32, -1.0, 1.0)
    return centre + 0.3 * spacing[:, None] * noise


def draw_counts(key, part):
    key = jax.random.fold_in(key, 23)
    drawn = jax.random.randint(key, (NX, NY, NZ), P_SIZE // 4, P_SIZE + 1, jnp.int32)
    return drawn.at[0, 0, 0].set(P_SIZE)


def with_ends(values, key, smallest, high):
    spot = [jax.random.randint(jax.random.fold_in(key, axis), (), 0, length) for axis, length in enumerate(values.shape)]
    widest = values.shape.index(max(values.shape))
    neighbour = spot[:widest] + [(spot[widest] + 1) % values.shape[widest]] + spot[widest + 1:]
    return values.at[tuple(spot)].set(smallest).at[tuple(neighbour)].set(high)


def levels(rng, extent, split, smallest, top_value):
    gain = 1.0
    for axis_at, blocks in split:
        draws = jax.random.uniform(jax.random.fold_in(jax.random.fold_in(rng, 6), axis_at), (blocks,), jnp.float32, smallest / len(split), top_value / len(split))
        gain = gain * jnp.repeat(jnp.exp(draws), extent[axis_at] // blocks).reshape((-1,) + (1,) * (len(extent) - 1 - axis_at))
    return gain


def gaussian(own_key, dims, scale, most, shards=(), held_as=jnp.bfloat16):
    entries = scale * jax.random.normal(own_key, dims, jnp.float32)
    if shards:
        entries = entries * levels(own_key, dims, shards, -0.22, 0.18)
    return jnp.clip(entries, -most, most).astype(held_as)


def setup_inputs(seed: int = 0) -> dict:
    streams_of = jax.random.split(jax.random.key(seed), 9)
    return {
        "features": gaussian(streams_of[0], (NX, NY, NZ, P_SIZE, K), 1.0, 6.0, ((0, 16), (1, 4), (2, 4))),
        "positions": draw_positions(jax.random.fold_in(streams_of[8], 71), 0),
        "counts": draw_counts(jax.random.fold_in(streams_of[8], 71), 0),
        "species": with_ends(jax.random.randint(streams_of[3], (NX, NY, NZ, P_SIZE), 0, SPECIES), jax.random.fold_in(streams_of[3], 1), 0, SPECIES - 1).astype(jnp.int32),
        "radial_weight": gaussian(streams_of[4], (NB, 3, K), (NB * 96) ** -0.5, 0.21875, (), jnp.float32),
        "mix_weight": gaussian(streams_of[5], (K, K), K ** -0.5, 0.5),
        "skip_weight": gaussian(streams_of[6], (SPECIES, K, K), K ** -0.5, 0.5),
        "readout": gaussian(streams_of[7], (SPECIES, K), 0.5, 3.0, (), jnp.float32),
    }


CUTOFF = 6.0
SENTINEL = 1000.0
SMALL = 1e-06
DEGREE = np.array([0, 1, 1, 1, 2, 2, 2, 2, 2])

def neighbour_offsets():
    shape = (3, 3, 3, 3, 1)
    first = lax.broadcasted_iota(jnp.int32, shape, 0)
    second = lax.broadcasted_iota(jnp.int32, shape, 1)
    third = lax.broadcasted_iota(jnp.int32, shape, 2)
    component = lax.broadcasted_iota(jnp.int32, shape, 3)
    picked = jnp.where(component == 0, first, jnp.where(component == 1, second, third))
    return (picked - 1).astype(jnp.float32) * CUTOFF

def cell_grid(size_x, size_y, size_z):
    flat = jnp.arange(size_x * size_y * size_z, dtype=jnp.int32)
    return jnp.stack([flat // (size_y * size_z), flat // size_z % size_y, flat % size_z], 1).astype(jnp.int32)

def harmonics(unit):
    unit_x, unit_y, unit_z = (unit[0], unit[1], unit[2])
    root3 = math.sqrt(3.0)
    root5 = math.sqrt(5.0)
    root15 = math.sqrt(15.0)
    return jnp.stack([jnp.ones_like(unit_x), root3 * unit_x, root3 * unit_y, root3 * unit_z, root15 * unit_x * unit_y, root15 * unit_y * unit_z, 0.5 * root5 * (3.0 * unit_z * unit_z - 1.0), root15 * unit_x * unit_z, 0.5 * root15 * (unit_x * unit_x - unit_y * unit_y)])

def pair_table(near_pos, own_pos, nbasis):
    slots = own_pos.shape[1]
    width = near_pos.shape[1]
    delta = near_pos[:, None, :] - own_pos[:, :, None]
    radius = jnp.sqrt(lax.optimization_barrier(jnp.sum(delta * delta, 0)) + SMALL)
    unit = delta / radius
    scaled = radius / CUTOFF
    envelope = jnp.where(scaled < 1.0, 1.0 - 28.0 * scaled ** 6 + 48.0 * scaled ** 7 - 21.0 * scaled ** 8, 0.0)
    column = lax.broadcasted_iota(jnp.int32, (slots, width), 1)
    row_index = lax.broadcasted_iota(jnp.int32, (slots, width), 0)
    keeper = jnp.where(column == 13 * slots + row_index, 0.0, envelope)
    freqs = jnp.arange(1, nbasis + 1).astype(jnp.float32) * math.pi
    radial = math.sqrt(2.0 / CUTOFF) * jnp.sin(freqs[:, None, None] * scaled[None]) / radius[None] * keeper[None]
    table = radial[:, None] * harmonics(unit)[None]
    return table.reshape(nbasis * 9 * slots, width).astype(jnp.bfloat16)

def cell_terms(feat_ext, pos_ext, corner, kinds, alive, radial_weight, mix_weight, skip_weight, readout, table_fn):
    slots = feat_ext.shape[3]
    chans = feat_ext.shape[4]
    nbasis = radial_weight.shape[0]
    nspecies = readout.shape[0]
    zero = jnp.zeros((), jnp.int32)
    feat_block = lax.dynamic_slice(feat_ext, (corner[0], corner[1], corner[2], zero, zero), (3, 3, 3, slots, chans))
    pos_block = lax.dynamic_slice(pos_ext, (corner[0], corner[1], corner[2], zero, zero), (3, 3, 3, 3, slots))
    pos_block = pos_block + neighbour_offsets()
    own_feat = feat_block[1, 1, 1].astype(jnp.bfloat16)
    near_feat = feat_block.reshape(27 * slots, chans).astype(jnp.bfloat16)
    own_pos = pos_block[1, 1, 1]
    near_pos = jnp.transpose(pos_block, (3, 0, 1, 2, 4)).reshape(3, 27 * slots)
    table = table_fn(near_pos, own_pos)
    dens = jnp.dot(table, near_feat, preferred_element_type=jnp.float32).reshape(nbasis, 9, slots, chans)
    per_comp = radial_weight[:, DEGREE, :]
    moments = jnp.einsum('bmpk,bmk->mpk', dens, per_comp, precision=lax.Precision.HIGHEST)
    product = moments[0] + lax.optimization_barrier(jnp.sum(moments[1:4] ** 2, 0)) + lax.optimization_barrier(jnp.sum(moments[4:] ** 2, 0))
    product = product.astype(jnp.bfloat16)
    onehot = (kinds[:, None] == jnp.arange(nspecies, dtype=jnp.int32)[None, :]).astype(jnp.float32)
    updated = jnp.dot(product, mix_weight, preferred_element_type=jnp.float32)
    for kind in range(nspecies):
        updated = updated + onehot[:, kind:kind + 1] * jnp.dot(own_feat, skip_weight[kind], preferred_element_type=jnp.float32)
    chosen = jnp.dot(onehot, readout, precision=lax.Precision.HIGHEST)
    energy = jnp.sum(alive * lax.optimization_barrier(jnp.sum(chosen * jax.nn.silu(updated), 1)))
    return (energy, updated)

def wrap_pad(array, fill):
    array = jnp.concatenate([array[-1:], array, array[:1]], 0)
    array = jnp.concatenate([array[:, -1:], array, array[:, :1]], 1)
    layer = jnp.full_like(array[:, :, :1], fill)
    return jnp.concatenate([layer, array, layer], 2)

def reference(features, positions, counts, species, radial_weight, mix_weight, skip_weight, readout):
    live = (lax.broadcasted_iota(jnp.int32, (NX, NY, NZ, P_SIZE), 3) < counts[..., None]).astype(jnp.float32)
    moved = jnp.where(live[:, :, :, None, :] > 0, positions, SENTINEL)
    feat32 = features.astype(jnp.float32)
    grid = cell_grid(NX, NY, NZ)
    kinds_flat = species.reshape(-1, P_SIZE)
    alive_flat = live.reshape(-1, P_SIZE)
    table_fn = partial(pair_table, nbasis=NB)

    def total(feat_all, pos_all):
        feat_ext = wrap_pad(feat_all, 0.0)
        pos_ext = wrap_pad(pos_all, SENTINEL)

        def per_cell(item):
            return cell_terms(feat_ext, pos_ext, item[0], item[1], item[2], radial_weight, mix_weight, skip_weight, readout, table_fn)
        energies, updated = lax.map(jax.checkpoint(per_cell), (grid, kinds_flat, alive_flat))
        return (jnp.sum(energies), updated)
    energy, pullback, updated = jax.vjp(total, feat32, moved, has_aux=True)
    grad_feat, grad_pos = pullback(jnp.ones((), jnp.float32))
    new_features = (updated.reshape(NX, NY, NZ, P_SIZE, K) * live[..., None]).astype(jnp.bfloat16)
    forces = -grad_pos * live[:, :, :, None, :]
    return (new_features, forces, grad_feat)
```

```python
from functools import partial
import math

import jax
import jax.numpy as jnp
from jax import lax
from jax.experimental import pallas as pl
from jax.experimental.pallas import tpu as pltpu
from jax.sharding import PartitionSpec as P

CUTOFF = 6.0
SENTINEL = 1000.0
SMALL = 1e-06
K = 128
NB = 8
NM = 9
SPECIES = 5
SLOTS = 32
CELLS = 8
DEG = (0, 1, 1, 1, 2, 2, 2, 2, 2)
OWN = CELLS * SLOTS
GHOSTS = 19
GWIDTH = 640
ROW = SLOTS + 16
HALF = NB * NM * 16
ROWS = 2 * HALF
F32 = jnp.float32
BF16 = jnp.bfloat16
ROOT3, ROOT5, ROOT15 = math.sqrt(3.0), math.sqrt(5.0), math.sqrt(15.0)
NORM = math.sqrt(2.0 / CUTOFF)
COS_FIT = (3.999999997, -3.739208102, 1.277990829, -0.2287452958, 0.02416752431)
SIN_FIT = (3.141592654, -5.167712765, 2.550163319, -0.5992521978, 0.08205040168, -0.00702838621)
GHOST_LIST = tuple(
    (a, b, c) for a in range(3) for b in range(3) for c in range(3) if 2 in (a, b, c)
)


def horner(coefs, y):
    acc = jnp.full_like(y, coefs[-1])
    for value in coefs[-2::-1]:
        acc = acc * y + value
    return acc


def pair_geometry(near, own, self_lane):
    dx, dy, dz = (near[k] - own[k] for k in range(3))
    inv = lax.rsqrt(dx * dx + dy * dy + dz * dz + SMALL)
    r2 = dx * dx + dy * dy + dz * dz + SMALL
    s = jnp.minimum(r2 * inv * (1.0 / CUTOFF), 1.0)
    ux, uy, uz = dx * inv, dy * inv, dz * inv
    t = 0.5 - s
    y = t * t
    first = (1.0 - s) * horner(COS_FIT, y) * (NORM / CUTOFF)
    cosine = t * horner(SIN_FIT, y)
    s2 = s * s
    s5 = s2 * s2 * s
    env = 1.0 - s5 * s * (28.0 - 48.0 * s + 21.0 * s2)
    away = 1.0 - s
    denv = s5 * (away * away) * (-168.0 / CUTOFF)
    if self_lane is not None:
        lane = lax.broadcasted_iota(jnp.int32, dx.shape, 1)
        row = lax.broadcasted_iota(jnp.int32, dx.shape, 0)
        same = lane == row + self_lane
        env = jnp.where(same, 0.0, env)
        denv = jnp.where(same, 0.0, denv)
    return inv, ux, uy, uz, first, cosine, env, denv


def sine_series(first, cosine):
    twice = cosine + cosine
    out = [first, twice * first]
    for _ in range(NB - 2):
        out.append(twice * out[-1] - out[-2])
    return out


def cosine_series(cosine):
    twice = cosine + cosine
    out = [cosine, twice * cosine - 1.0]
    for _ in range(NB - 2):
        out.append(twice * out[-1] - out[-2])
    return [float(b + 1) * value for b, value in enumerate(out)]


def harmonics(ux, uy, uz):
    return [
        None,
        ROOT3 * ux,
        ROOT3 * uy,
        ROOT3 * uz,
        ROOT15 * ux * uy,
        ROOT15 * uy * uz,
        0.5 * ROOT5 * (3.0 * uz * uz - 1.0),
        ROOT15 * ux * uz,
        0.5 * ROOT15 * (ux * ux - uy * uy),
    ]


def lane_to_rows(line):
    return jnp.broadcast_to(line, (128, 128)).T


def contract_last(a, b):
    return lax.dot_general(a, b, (((1,), (1,)), ((), ())), preferred_element_type=F32)


def flat(x, y, z):
    return x * 16 + y * 4 + z


def own_xyz(cell):
    return cell // 4, (cell // 2) % 2, cell % 2


def tail_of(rows):
    index = lax.broadcasted_iota(jnp.int32, (16, 128), 0)
    tail = jnp.zeros((16, 128), F32)
    for k, line in enumerate(rows):
        tail = jnp.where(index == k, jnp.broadcast_to(line, (16, 128)), tail)
    return tail.astype(BF16)


def split_line(line, pieces):
    out = []
    for _ in range(pieces):
        part = line.astype(BF16).astype(F32)
        out.append(part)
        line = line - part
    return out


def line_of(ref, cell, pieces):
    tail = ref[cell, SLOTS:ROW, :].astype(F32)
    line = tail[0:1, :]
    for k in range(1, pieces):
        line = line + tail[k : k + 1, :]
    return line


def ext_source(x, y, z, own, xlo, xhi, ylo, yhi, zlo, zhi):
    if z in (0, 3):
        return (zlo if z == 0 else zhi), x * 4 + y
    if y in (0, 3):
        return (ylo if y == 0 else yhi), x * 2 + z - 1
    if x in (0, 3):
        return (xlo if x == 0 else xhi), (y - 1) * 2 + z - 1
    return own, (x - 1) * 4 + (y - 1) * 2 + z - 1


def pack_x_kernel(counts_ref, feat_ref, pos_ref, own_ref, xlo_ref, xhi_ref, line_ref):
    lane = lax.broadcasted_iota(jnp.int32, (1, SLOTS), 1)
    line_ref[...] = jnp.zeros_like(line_ref)
    for c in range(CELLS):
        for k in range(3):
            x, y, z = own_xyz(c)
            value = pos_ref[x, y, k, z : z + 1, :]
            value = jnp.where(lane < counts_ref[x, y, z], value, SENTINEL)
            line_ref[c : c + 1, k * SLOTS : (k + 1) * SLOTS] = value
    pieces = split_line(line_ref[...], 3)
    for c in range(CELLS):
        tail = tail_of([piece[c : c + 1, :] for piece in pieces])
        feat = feat_ref[c]
        for ref, spot in ((own_ref, c), ((xlo_ref, xhi_ref)[c // 4], c % 4)):
            ref[spot, 0:SLOTS, :] = feat
            ref[spot, SLOTS:ROW, :] = tail


def pack_y_kernel(own, xlo, xhi, lo_ref, hi_ref):
    for y, ref in ((1, lo_ref), (2, hi_ref)):
        for x in range(4):
            for z in (1, 2):
                source, spot = ext_source(x, y, z, own, xlo, xhi, None, None, None, None)
                ref[x * 2 + z - 1] = source[spot]


def pack_z_kernel(own, xlo, xhi, ylo, yhi, lo_ref, hi_ref):
    for z, ref in ((1, lo_ref), (2, hi_ref)):
        for x in range(4):
            for y in range(4):
                source, spot = ext_source(x, y, z, own, xlo, xhi, ylo, yhi, None, None)
                ref[x * 4 + y] = source[spot]


def load_own(own_ref, nf_ref, near_ref, ownpos_ref):
    for c in range(CELLS):
        nf_ref[c * SLOTS : (c + 1) * SLOTS, :] = own_ref[c, 0:SLOTS, :]
        line = line_of(own_ref, c, 3)
        for k, spot in enumerate(own_xyz(c)):
            moved = line[:, k * SLOTS : (k + 1) * SLOTS] + (spot + 1) * CUTOFF
            near_ref[k : k + 1, c * SLOTS : (c + 1) * SLOTS] = moved
    for half in range(2):
        lanes = slice(half * 128, half * 128 + 128)
        for k in range(3):
            ownpos_ref[k, lanes, :] = lane_to_rows(near_ref[k : k + 1, lanes])


def geometry_of(near_ref, ownpos_ref, cell, block, tile, own_pairs):
    lanes = slice(tile * 128, tile * 128 + 128)
    near = [near_ref[k : k + 1, lanes] for k in range(3)]
    start = pl.multiple_of(cell * SLOTS + block * 16, 16)
    own = [ownpos_ref[k, pl.ds(start, 16), :] for k in range(3)]
    return pair_geometry(near, own, start - tile * 128 if own_pairs else None)


def build_table(table_ref, geometry, tiles):
    for tile in range(tiles):
        lanes = slice(tile * 128, tile * 128 + 128)
        for block in range(2):
            inv, ux, uy, uz, first, cosine, env, denv = geometry(block, tile)
            radial = [value * env for value in sine_series(first, cosine)]
            shape = harmonics(ux, uy, uz)
            for b in range(NB):
                for m in range(NM):
                    row = block * HALF + (b * NM + m) * 16
                    value = radial[b] if m == 0 else radial[b] * shape[m]
                    table_ref[row : row + 16, lanes] = value.astype(BF16)


def weigh(dens_ref, rw_ref, block, m):
    total = None
    for b in range(NB):
        row = block * HALF + (b * NM + m) * 16
        weight = rw_ref[DEG[m], b : b + 1, :]
        term = dens_ref[row : row + 16, :] * weight
        total = term if total is None else total + term
    return total


def spread(mom_ref, cell, rw_ref, dd_ref):
    for block in range(2):
        for m in range(NM):
            cot = mom_ref[cell, m, block * 16 : block * 16 + 16, :]
            for b in range(NB):
                row = block * HALF + (b * NM + m) * 16
                weight = rw_ref[DEG[m], b : b + 1, :]
                dd_ref[row : row + 16, :] = (cot * weight).astype(BF16)


def pair_forces(geometry, dd_ref, nf_ref, dt_ref, width, near_out, fown_ref):
    pulls = [[None] * 3, [None] * 3]
    for chunk in range((width + 255) // 256):
        low = chunk * 256
        high = min(low + 256, width)
        slab = dt_ref.at[chunk % 2]
        slab[:, : high - low] = contract_last(dd_ref[...], nf_ref[low:high, :])
        for tile in range(low // 128, high // 128):
            inside = slice(tile * 128 - low, tile * 128 - low + 128)
            near_sum = [None] * 3
            for block in range(2):
                inv, ux, uy, uz, first, cosine, env, denv = geometry(block, tile)
                sines = sine_series(first, cosine)
                cosines = cosine_series(cosine)
                shape = harmonics(ux, uy, uz)
                pull = [None] * NM
                total_s = None
                total_c = None
                for m in range(NM):
                    part_s = None
                    part_c = None
                    for b in range(NB):
                        row = block * HALF + (b * NM + m) * 16
                        value = slab[row : row + 16, inside]
                        one, two = value * sines[b], value * cosines[b]
                        part_s = one if part_s is None else part_s + one
                        part_c = two if part_c is None else part_c + two
                    pull[m] = part_s
                    if m == 0:
                        total_s, total_c = part_s, part_c
                    else:
                        total_s = total_s + part_s * shape[m]
                        total_c = total_c + part_c * shape[m]
                gx = ROOT3 * pull[1] + ROOT15 * (uy * pull[4] + uz * pull[7] + ux * pull[8])
                gy = ROOT3 * pull[2] + ROOT15 * (ux * pull[4] + uz * pull[5] - uy * pull[8])
                gz = (
                    ROOT3 * pull[3]
                    + ROOT15 * (uy * pull[5] + ux * pull[7])
                    + (3.0 * ROOT5) * uz * pull[6]
                )
                scale = env * inv
                turn = ux * gx + uy * gy + uz * gz
                wave = (math.pi / CUTOFF * NORM) * total_c
                along = denv * total_s + scale * (wave - total_s - turn)
                for k, (unit, side) in enumerate(((ux, gx), (uy, gy), (uz, gz))):
                    force = unit * along + scale * side
                    near_sum[k] = force if block == 0 else near_sum[k] + force
                    held = pulls[block][k]
                    pulls[block][k] = force if held is None else held + force
            near_out(tile, [jnp.sum(value, axis=0, keepdims=True) for value in near_sum])
    for k in range(3):
        for block in range(2):
            fown_ref[k * SLOTS + block * 16 : k * SLOTS + block * 16 + 16, :] = pulls[block][k]
    return jnp.sum(fown_ref[...].T, axis=0, keepdims=True)


def own_forward_kernel(first, own_ref, rw_ref, mom_ref, nf_ref, near_ref, ownpos_ref, table_ref, dens_ref):
    load_own(own_ref, nf_ref, near_ref, ownpos_ref)

    def step(at, carry):
        cell = first + at
        build_table(table_ref, lambda b, t: geometry_of(near_ref, ownpos_ref, cell, b, t, True), 2)
        dens_ref[...] = jnp.dot(table_ref[...], nf_ref[...], preferred_element_type=F32)
        for block in range(2):
            for m in range(NM):
                mom_ref[at, m, block * 16 : block * 16 + 16, :] = weigh(dens_ref, rw_ref, block, m)
        return carry

    lax.fori_loop(0, mom_ref.shape[0], step, 0)


def own_backward_kernel(
    first, count, own_ref, rw_ref, mom_ref, gown_ref, lines_ref,
    nf_ref, near_ref, ownpos_ref, table_ref, dd_ref, dt_ref, gnear_ref, fown_ref, gsum_ref,
):
    load_own(own_ref, nf_ref, near_ref, ownpos_ref)
    gsum_ref[...] = jnp.zeros_like(gsum_ref)
    gnear_ref[...] = jnp.zeros_like(gnear_ref)
    fown_ref[...] = jnp.zeros_like(fown_ref)
    lines_ref[...] = jnp.zeros_like(lines_ref)

    def near_out(tile, sums):
        for k in range(3):
            gnear_ref[k : k + 1, tile * 128 : tile * 128 + 128] += sums[k]

    def step(at, carry):
        cell = first + at

        def geometry(block, tile):
            return geometry_of(near_ref, ownpos_ref, cell, block, tile, True)

        spread(mom_ref, cell, rw_ref, dd_ref)
        build_table(table_ref, geometry, 2)
        gsum_ref[...] += lax.dot_general(
            dd_ref[...], table_ref[...], (((0,), (0,)), ((), ())), preferred_element_type=F32
        )
        line = pair_forces(geometry, dd_ref, nf_ref, dt_ref, OWN, near_out, fown_ref)
        lines_ref[pl.ds(cell, 1), :] = -line
        return carry

    lax.fori_loop(0, count, step, 0)
    gown_ref[...] = gsum_ref[...].T
    for c in range(CELLS):
        for k in range(3):
            lanes = slice(k * SLOTS, (k + 1) * SLOTS)
            lines_ref[c : c + 1, lanes] += gnear_ref[k : k + 1, c * SLOTS : (c + 1) * SLOTS]


def ghost_kernel(
    parts, *refs
):
    counts_ref, edges_ref, own, xlo, xhi, ylo, yhi, zlo, zhi = refs[:9]
    refs = refs[1:]
    mom_in = refs[8 : 8 + parts]
    species_ref, rw_ref, mix_ref, skip_ref, readout_ref = refs[8 + parts : 13 + parts]
    new_ref, szlo, szhi, rest_ref, rlines_ref, cot_ref = refs[13 + parts : 19 + parts]
    (
        feat_ref, pos_ref, lines_ref, nf_ref, near_ref, ownnf_ref, ownnear_ref, ownpos_ref, kind_ref,
        table_ref, dens_ref, mom_ref, dd_ref, dt_ref, gnear_ref, fown_ref, gfeat_ref, gpos_ref, sline_ref, oline_ref,
    ) = refs[19 + parts :]
    load_own(own, ownnf_ref, ownnear_ref, ownpos_ref)
    for c in range(CELLS):
        sline_ref[0:1, c * SLOTS : (c + 1) * SLOTS] = species_ref[c : c + 1, :].astype(F32)
    for half in range(2):
        lanes = slice(half * 128, half * 128 + 128)
        kind_ref[lanes, :] = lane_to_rows(sline_ref[0:1, lanes])
    for x in range(4):
        for y in range(4):
            for z in range(4):
                source, spot = ext_source(x, y, z, own, xlo, xhi, ylo, yhi, zlo, zhi)
                cell = flat(x, y, z)
                feat_ref[cell] = source[spot, 0:SLOTS, :]
                lines_ref[cell : cell + 1, :] = line_of(source, spot, 3)
    index = lax.broadcasted_iota(jnp.int32, (64, SLOTS), 0)
    spots = (index >> 4, (index >> 2) & 3, index & 3)
    depth = spots[2]
    outside = ((depth == 0) & (edges_ref[0] > 0)) | ((depth == 3) & (edges_ref[1] > 0))
    for k in range(3):
        value = jnp.where(outside, SENTINEL, lines_ref[:, k * SLOTS : (k + 1) * SLOTS])
        pos_ref[k, :, 0:SLOTS] = value + spots[k].astype(F32) * CUTOFF
    spare = GWIDTH - GHOSTS * SLOTS
    near_ref[:, GHOSTS * SLOTS :] = jnp.full((8, spare), 5000.0, F32)
    nf_ref[GHOSTS * SLOTS :, :] = jnp.zeros((spare, K), BF16)
    gnear_ref[...] = jnp.zeros_like(gnear_ref)
    gfeat_ref[...] = jnp.zeros_like(gfeat_ref)
    gpos_ref[...] = jnp.zeros_like(gpos_ref)
    fown_ref[...] = jnp.zeros_like(fown_ref)
    oline_ref[...] = jnp.zeros_like(oline_ref)

    def ghost_cell(cell, which):
        return flat(*(3 * at if side == 2 else side + 1 for side, at in zip(which, own_xyz(cell))))

    def load_ghosts(cell):
        for g, which in enumerate(GHOST_LIST):
            spot = ghost_cell(cell, which)
            nf_ref[g * SLOTS : (g + 1) * SLOTS, :] = feat_ref[spot]
            for k in range(3):
                near_ref[k : k + 1, g * SLOTS : (g + 1) * SLOTS] = pos_ref[k, pl.ds(spot, 1), 0:SLOTS]

    def geometry_at(cell):
        return lambda block, tile: geometry_of(near_ref, ownpos_ref, cell, block, tile, False)

    at = 0
    for held in mom_in:
        mom_ref[at : at + held.shape[0]] = held[...]
        at += held.shape[0]

    def forward(cell, carry):
        load_ghosts(cell)
        build_table(table_ref.at[cell], geometry_at(cell), GWIDTH // 128)
        dens_ref[...] = jnp.dot(table_ref[cell], nf_ref[...], preferred_element_type=F32)
        for block in range(2):
            for m in range(NM):
                mom_ref[cell, m, block * 16 : block * 16 + 16, :] += weigh(dens_ref, rw_ref, block, m)
        return carry

    lax.fori_loop(0, CELLS, forward, 0)

    moments = [mom_ref[:, m].reshape(OWN, K) for m in range(NM)]
    product = moments[0]
    for m in range(1, NM):
        product = product + moments[m] * moments[m]
    own_feat = ownnf_ref[...]
    kinds = kind_ref[...]
    updated = jnp.dot(product.astype(BF16), mix_ref[...], preferred_element_type=F32)
    chosen = jnp.zeros((OWN, K), F32)
    for k in range(SPECIES):
        hot = kinds == float(k)
        masked = jnp.where(hot, own_feat.astype(F32), 0.0).astype(BF16)
        updated = updated + jnp.dot(masked, skip_ref[k], preferred_element_type=F32)
        chosen = jnp.where(hot, readout_ref[k : k + 1, :], chosen)
    slot = lax.broadcasted_iota(jnp.int32, (SLOTS, K), 0)
    alive = jnp.concatenate(
        [jnp.where(slot < counts_ref[own_xyz(c)], 1.0, 0.0) for c in range(CELLS)], axis=0
    )
    new_ref[...] = (updated * alive).astype(BF16)
    gate = 1.0 / (1.0 + jnp.exp(-updated))
    dupdated = alive * chosen * gate * (1.0 + updated * (1.0 - gate))
    dproduct = contract_last(dupdated.astype(BF16), mix_ref[...])
    dskip = jnp.zeros((OWN, K), F32)
    for k in range(SPECIES):
        masked = jnp.where(kinds == float(k), dupdated, 0.0).astype(BF16)
        dskip = dskip + contract_last(masked, skip_ref[k])
    for c in range(CELLS):
        x, y, z = own_xyz(c)
        gfeat_ref[flat(x + 1, y + 1, z + 1)] = dskip[c * SLOTS : (c + 1) * SLOTS, :]
    cot_ref[:, 0] = dproduct.reshape(CELLS, SLOTS, K)
    for m in range(1, NM):
        cot_ref[:, m] = (2.0 * moments[m] * dproduct).reshape(CELLS, SLOTS, K)

    def near_out(tile, sums):
        for k in range(3):
            gnear_ref[k : k + 1, tile * 128 : tile * 128 + 128] = sums[k]

    def backward(cell, carry):
        load_ghosts(cell)
        spread(cot_ref, cell, rw_ref, dd_ref)
        grads = lax.dot_general(
            dd_ref[...], table_ref[cell], (((0,), (0,)), ((), ())), preferred_element_type=F32
        ).T
        for g, which in enumerate(GHOST_LIST):
            gfeat_ref[ghost_cell(cell, which)] += grads[g * SLOTS : (g + 1) * SLOTS, :]
        line = pair_forces(geometry_at(cell), dd_ref, nf_ref, dt_ref, GWIDTH, near_out, fown_ref)
        oline_ref[pl.ds(cell, 1), :] = -line
        for g, which in enumerate(GHOST_LIST):
            spot = ghost_cell(cell, which)
            for k in range(3):
                gpos_ref[k, pl.ds(spot, 1), 0:SLOTS] += gnear_ref[
                    k : k + 1, g * SLOTS : (g + 1) * SLOTS
                ]
        return carry

    lax.fori_loop(0, CELLS, backward, 0)

    for k in range(3):
        lines_ref[:, k * SLOTS : (k + 1) * SLOTS] = gpos_ref[k, :, 0:SLOTS]
    for c in range(CELLS):
        cell = flat(*(at + 1 for at in own_xyz(c)))
        lines_ref[cell : cell + 1, :] = oline_ref[c : c + 1, :]
    pieces = split_line(lines_ref[...], 2)
    for x in range(4):
        for y in range(4):
            for z in (1, 2):
                at, cell = (x * 4 + y) * 2 + z - 1, flat(x, y, z)
                rest_ref[at] = gfeat_ref[cell]
                rlines_ref[at : at + 1, :] = lines_ref[cell : cell + 1, :]
            for z, ref in ((0, szlo), (3, szhi)):
                at, cell = x * 4 + y, flat(x, y, z)
                ref[at, 0:SLOTS, :] = gfeat_ref[cell].astype(BF16)
                ref[at, SLOTS:ROW, :] = tail_of([piece[cell : cell + 1, :] for piece in pieces])


def gathered(x, y, z, rest_ref, rlines_ref, zs, ys, xs):
    at = (x * 4 + y) * 2 + z - 1
    feat = rest_ref[at]
    line = rlines_ref[at : at + 1, :]
    for faces, side, spot in (
        (zs, z, x * 4 + y),
        (ys, y, x * 2 + z - 1),
        (xs, x, (y - 1) * 2 + z - 1),
    ):
        if faces is not None:
            ref = faces[side - 1]
            feat = feat + ref[spot, 0:SLOTS, :].astype(F32)
            line = line + line_of(ref, spot, 2)
    return feat, line


def back_y_kernel(rest_ref, rlines_ref, zlo, zhi, lo_ref, hi_ref):
    for y, ref in ((0, lo_ref), (3, hi_ref)):
        for x in range(4):
            for z in (1, 2):
                feat, line = gathered(x, y, z, rest_ref, rlines_ref, (zlo, zhi), None, None)
                spot = x * 2 + z - 1
                ref[spot, 0:SLOTS, :] = feat.astype(BF16)
                ref[spot, SLOTS:ROW, :] = tail_of(split_line(line, 2))


def back_x_kernel(rest_ref, rlines_ref, zlo, zhi, ylo, yhi, lo_ref, hi_ref):
    for x, ref in ((0, lo_ref), (3, hi_ref)):
        for y in (1, 2):
            for z in (1, 2):
                feat, line = gathered(x, y, z, rest_ref, rlines_ref, (zlo, zhi), (ylo, yhi), None)
                spot = (y - 1) * 2 + z - 1
                ref[spot, 0:SLOTS, :] = feat.astype(BF16)
                ref[spot, SLOTS:ROW, :] = tail_of(split_line(line, 2))


def finish_kernel(parts, *refs):
    counts_ref, rest_ref, rlines_ref, zlo, zhi, ylo, yhi, xlo, xhi = refs[:9]
    gowns, lines = refs[9 : 9 + parts], refs[9 + parts : 9 + 2 * parts]
    grad_ref, force_ref = refs[9 + 2 * parts :]
    lane = lax.broadcasted_iota(jnp.int32, (1, SLOTS), 1)
    for c in range(CELLS):
        x, y, z = (at + 1 for at in own_xyz(c))
        feat, line = gathered(x, y, z, rest_ref, rlines_ref, (zlo, zhi), (ylo, yhi), (xlo, xhi))
        for gown, own_line in zip(gowns, lines):
            feat = feat + gown[c * SLOTS : (c + 1) * SLOTS, :]
            line = line + own_line[c : c + 1, :]
        grad_ref[c] = feat
        for k in range(3):
            x, y, z = own_xyz(c)
            force = jnp.where(lane < counts_ref[x, y, z], -line[:, k * SLOTS : (k + 1) * SLOTS], 0.0)
            force_ref[x, y, k, z : z + 1, :] = force


VMEM_SPEC = pl.BlockSpec(memory_space=pltpu.VMEM)
SMEM_SPEC = pl.BlockSpec(memory_space=pltpu.SMEM)


def call(kernel, name, shapes, args, scalars=0, scratch=(), limit=16, flops=0):
    out_shape = tuple(jax.ShapeDtypeStruct(shape, dtype) for shape, dtype in shapes)
    return pl.pallas_call(
        kernel,
        out_shape=out_shape,
        in_specs=[SMEM_SPEC] * scalars + [VMEM_SPEC] * (len(args) - scalars),
        out_specs=tuple(VMEM_SPEC for _ in shapes),
        scratch_shapes=list(scratch),
        compiler_params=pltpu.CompilerParams(vmem_limit_bytes=limit * 1024 * 1024),
        cost_estimate=pl.CostEstimate(flops=flops, bytes_accessed=1 << 20, transcendentals=0),
        name=name,
    )(*args)


def faces(cells):
    return [((cells, ROW, K), BF16)] * 2


def own_forward(own, rw, first, count):
    return call(
        partial(own_forward_kernel, first),
        "own_forward",
        [((count, NM, SLOTS, K), F32)],
        (own, rw),
        scratch=[
            pltpu.VMEM((OWN, K), BF16),
            pltpu.VMEM((8, OWN), F32),
            pltpu.VMEM((3, OWN, 128), F32),
            pltpu.VMEM((ROWS, OWN), BF16),
            pltpu.VMEM((ROWS, K), F32),
        ],
        flops=8 * count * ROWS * OWN * K,
    )[0]


def own_backward(own, rw, cot, first, count):
    return call(
        partial(own_backward_kernel, first, count),
        "own_backward",
        [((OWN, K), F32), ((CELLS, 128), F32)],
        (own, rw, cot),
        scratch=[
            pltpu.VMEM((OWN, K), BF16),
            pltpu.VMEM((8, OWN), F32),
            pltpu.VMEM((3, OWN, 128), F32),
            pltpu.VMEM((ROWS, OWN), BF16),
            pltpu.VMEM((ROWS, K), BF16),
            pltpu.VMEM((1, ROWS, 256), F32),
            pltpu.VMEM((8, OWN), F32),
            pltpu.VMEM((128, 128), F32),
            pltpu.VMEM((K, OWN), F32),
        ],
        flops=16 * count * ROWS * OWN * K,
    )


def ghost(counts, edges, payloads, moms, species, rw, mix, skip, readout):
    return call(
        partial(ghost_kernel, len(moms)),
        "ghost",
        [((OWN, K), BF16)]
        + faces(16)
        + [((32, SLOTS, K), F32), ((32, 128), F32), ((CELLS, NM, SLOTS, K), F32)],
        (counts, edges, *payloads, *moms, species, rw, mix, skip, readout),
        scalars=2,
        scratch=[
            pltpu.VMEM((64, SLOTS, K), BF16),
            pltpu.VMEM((3, 64, 128), F32),
            pltpu.VMEM((64, 128), F32),
            pltpu.VMEM((GWIDTH, K), BF16),
            pltpu.VMEM((8, GWIDTH), F32),
            pltpu.VMEM((OWN, K), BF16),
            pltpu.VMEM((8, OWN), F32),
            pltpu.VMEM((3, OWN, 128), F32),
            pltpu.VMEM((OWN, 128), F32),
            pltpu.VMEM((CELLS, ROWS, GWIDTH), BF16),
            pltpu.VMEM((ROWS, K), F32),
            pltpu.VMEM((CELLS, NM, SLOTS, K), F32),
            pltpu.VMEM((ROWS, K), BF16),
            pltpu.VMEM((2, ROWS, 256), F32),
            pltpu.VMEM((8, GWIDTH), F32),
            pltpu.VMEM((128, 128), F32),
            pltpu.VMEM((64, SLOTS, K), F32),
            pltpu.VMEM((3, 64, 128), F32),
            pltpu.VMEM((8, OWN), F32),
            pltpu.VMEM((CELLS, 128), F32),
        ],
        limit=40,
        flops=16 * CELLS * ROWS * GWIDTH * K,
    )


def moved(lo, hi, axis, ring):
    size = lax.axis_size(axis)
    up = [(i, (i + 1) % size) for i in range(size if ring else size - 1)]
    down = [(j, i) for i, j in up]
    return lax.ppermute(hi, axis, up), lax.ppermute(lo, axis, down)


FORWARD_PARTS = ((0, 2), (2, 2), (4, 4))
BACKWARD_PARTS = ((0, 4), (4, 2), (6, 2))


def after(values, done):
    return lax.optimization_barrier((values, done))[0]


def shards(features, positions, counts, species, radial_weight, mix_weight, skip_weight, readout):
    plane = lax.axis_index("gz")
    edges = jnp.stack([plane == 0, plane == lax.axis_size("gz") - 1]).astype(jnp.int32)
    rw = jnp.transpose(radial_weight, (1, 0, 2))
    own, xlo, xhi = call(
        pack_x_kernel,
        "pack_x",
        [((CELLS, ROW, K), BF16)] + faces(4),
        (counts, features.reshape(CELLS, SLOTS, K), jnp.transpose(positions, (0, 1, 3, 2, 4))),
        scalars=1,
        scratch=[pltpu.VMEM((CELLS, 128), F32)],
    )
    xs = moved(xlo, xhi, "gx", True)
    moms = [own_forward(own, rw, *FORWARD_PARTS[0])]
    xs = after(xs, moms[0])
    ylo, yhi = call(pack_y_kernel, "pack_y", faces(8), (own, *xs))
    ys = moved(ylo, yhi, "gy", True)
    moms.append(own_forward(after(own, ylo), rw, *FORWARD_PARTS[1]))
    ys = after(ys, moms[1])
    zlo, zhi = call(pack_z_kernel, "pack_z", faces(16), (own, *xs, *ys))
    zs = moved(zlo, zhi, "gz", False)
    moms.append(own_forward(after(own, zlo), rw, *FORWARD_PARTS[2]))
    new, bzlo, bzhi, rest, rlines, cot = ghost(
        counts,
        edges,
        (own, *xs, *ys, *zs),
        moms,
        species.reshape(CELLS, SLOTS),
        rw,
        mix_weight,
        skip_weight,
        readout,
    )
    zs = moved(bzlo, bzhi, "gz", False)
    backs = [own_backward(own, rw, cot, *BACKWARD_PARTS[0])]
    zs = after(zs, backs[0][0])
    bylo, byhi = call(back_y_kernel, "back_y", faces(8), (rest, rlines, *zs))
    ys = moved(bylo, byhi, "gy", True)
    backs.append(own_backward(after(own, bylo), rw, cot, *BACKWARD_PARTS[1]))
    ys = after(ys, backs[1][0])
    bxlo, bxhi = call(back_x_kernel, "back_x", faces(4), (rest, rlines, *zs, *ys))
    xs = moved(bxlo, bxhi, "gx", True)
    backs.append(own_backward(after(own, bxlo), rw, cot, *BACKWARD_PARTS[2]))
    grad, force = call(
        partial(finish_kernel, len(backs)),
        "finish",
        [((CELLS, SLOTS, K), F32), ((2, 2, 3, 2, SLOTS), F32)],
        (counts, rest, rlines, *zs, *ys, *xs, *(b[0] for b in backs), *(b[1] for b in backs)),
        scalars=1,
    )
    return (
        new.reshape(2, 2, 2, SLOTS, K),
        jnp.transpose(force, (0, 1, 3, 2, 4)),
        grad.reshape(2, 2, 2, SLOTS, K),
    )


def solution(mesh):
    cells = P("gx", "gy", "gz", None, None)
    return jax.shard_map(
        shards,
        mesh=mesh,
        in_specs=(cells, cells, P("gx", "gy", "gz"), P("gx", "gy", "gz", None), P(), P(), P(), P()),
        out_specs=(cells, cells, cells),
        check_vma=False,
    )
```

```python
from functools import partial
import math

import jax
import jax.numpy as jnp
from jax import lax
from jax.experimental import pallas as pl
from jax.experimental.pallas import tpu as pltpu
from jax.sharding import PartitionSpec as P

CUTOFF = 6.0
SENTINEL = 1000.0
SMALL = 1e-06
K = 128
NB = 8
NM = 9
SPECIES = 5
SLOTS = 32
CELLS = 8
DEG = (0, 1, 1, 1, 2, 2, 2, 2, 2)
OWN = CELLS * SLOTS
GHOSTS = 19
GWIDTH = 640
ROW = SLOTS + 16
HALF = NB * NM * 16
ROWS = 2 * HALF
F32 = jnp.float32
BF16 = jnp.bfloat16
ROOT3, ROOT5, ROOT15 = math.sqrt(3.0), math.sqrt(5.0), math.sqrt(15.0)
NORM = math.sqrt(2.0 / CUTOFF)
COS_FIT = (3.999999997, -3.739208102, 1.277990829, -0.2287452958, 0.02416752431)
SIN_FIT = (3.141592654, -5.167712765, 2.550163319, -0.5992521978, 0.08205040168, -0.00702838621)
GHOST_LIST = tuple(
    (a, b, c) for a in range(3) for b in range(3) for c in range(3) if 2 in (a, b, c)
)


def horner(coefs, y):
    acc = jnp.full_like(y, coefs[-1])
    for value in coefs[-2::-1]:
        acc = acc * y + value
    return acc


def pair_geometry(near, own, self_lane):
    dx, dy, dz = (near[k] - own[k] for k in range(3))
    inv = lax.rsqrt(dx * dx + dy * dy + dz * dz + SMALL)
    r2 = dx * dx + dy * dy + dz * dz + SMALL
    s = jnp.minimum(r2 * inv * (1.0 / CUTOFF), 1.0)
    ux, uy, uz = dx * inv, dy * inv, dz * inv
    t = 0.5 - s
    y = t * t
    first = (1.0 - s) * horner(COS_FIT, y) * (NORM / CUTOFF)
    cosine = t * horner(SIN_FIT, y)
    s2 = s * s
    s5 = s2 * s2 * s
    env = 1.0 - s5 * s * (28.0 - 48.0 * s + 21.0 * s2)
    away = 1.0 - s
    denv = s5 * (away * away) * (-168.0 / CUTOFF)
    if self_lane is not None:
        lane = lax.broadcasted_iota(jnp.int32, dx.shape, 1)
        row = lax.broadcasted_iota(jnp.int32, dx.shape, 0)
        same = lane == row + self_lane
        env = jnp.where(same, 0.0, env)
        denv = jnp.where(same, 0.0, denv)
    return inv, ux, uy, uz, first, cosine, env, denv


def sine_series(first, cosine):
    twice = cosine + cosine
    out = [first, twice * first]
    for _ in range(NB - 2):
        out.append(twice * out[-1] - out[-2])
    return out


def cosine_series(cosine):
    twice = cosine + cosine
    out = [cosine, twice * cosine - 1.0]
    for _ in range(NB - 2):
        out.append(twice * out[-1] - out[-2])
    return [float(b + 1) * value for b, value in enumerate(out)]


def harmonics(ux, uy, uz):
    return [
        None,
        ROOT3 * ux,
        ROOT3 * uy,
        ROOT3 * uz,
        ROOT15 * ux * uy,
        ROOT15 * uy * uz,
        0.5 * ROOT5 * (3.0 * uz * uz - 1.0),
        ROOT15 * ux * uz,
        0.5 * ROOT15 * (ux * ux - uy * uy),
    ]


def lane_to_rows(line):
    return jnp.broadcast_to(line, (128, 128)).T


def contract_last(a, b):
    return lax.dot_general(a, b, (((1,), (1,)), ((), ())), preferred_element_type=F32)


def flat(x, y, z):
    return x * 16 + y * 4 + z


def own_xyz(cell):
    return cell // 4, (cell // 2) % 2, cell % 2


def tail_of(rows):
    index = lax.broadcasted_iota(jnp.int32, (16, 128), 0)
    tail = jnp.zeros((16, 128), F32)
    for k, line in enumerate(rows):
        tail = jnp.where(index == k, jnp.broadcast_to(line, (16, 128)), tail)
    return tail.astype(BF16)


def split_line(line, pieces):
    out = []
    for _ in range(pieces):
        part = line.astype(BF16).astype(F32)
        out.append(part)
        line = line - part
    return out


def line_of(ref, cell, pieces):
    tail = ref[cell, SLOTS:ROW, :].astype(F32)
    line = tail[0:1, :]
    for k in range(1, pieces):
        line = line + tail[k : k + 1, :]
    return line


def ext_source(x, y, z, own, xlo, xhi, ylo, yhi, zlo, zhi):
    if z in (0, 3):
        return (zlo if z == 0 else zhi), x * 4 + y
    if y in (0, 3):
        return (ylo if y == 0 else yhi), x * 2 + z - 1
    if x in (0, 3):
        return (xlo if x == 0 else xhi), (y - 1) * 2 + z - 1
    return own, (x - 1) * 4 + (y - 1) * 2 + z - 1


def pack_x_kernel(counts_ref, feat_ref, pos_ref, own_ref, xlo_ref, xhi_ref, line_ref):
    lane = lax.broadcasted_iota(jnp.int32, (1, SLOTS), 1)
    line_ref[...] = jnp.zeros_like(line_ref)
    for c in range(CELLS):
        for k in range(3):
            x, y, z = own_xyz(c)
            value = pos_ref[x, y, k, z : z + 1, :]
            value = jnp.where(lane < counts_ref[x, y : y + 1, z : z + 1], value, SENTINEL)
            line_ref[c : c + 1, k * SLOTS : (k + 1) * SLOTS] = value
    pieces = split_line(line_ref[...], 3)
    for c in range(CELLS):
        tail = tail_of([piece[c : c + 1, :] for piece in pieces])
        feat = feat_ref[c]
        for ref, spot in ((own_ref, c), ((xlo_ref, xhi_ref)[c // 4], c % 4)):
            ref[spot, 0:SLOTS, :] = feat
            ref[spot, SLOTS:ROW, :] = tail


def pack_y_kernel(own, xlo, xhi, lo_ref, hi_ref):
    for y, ref in ((1, lo_ref), (2, hi_ref)):
        for x in range(4):
            for z in (1, 2):
                source, spot = ext_source(x, y, z, own, xlo, xhi, None, None, None, None)
                ref[x * 2 + z - 1] = source[spot]


def pack_z_kernel(own, xlo, xhi, ylo, yhi, lo_ref, hi_ref):
    for z, ref in ((1, lo_ref), (2, hi_ref)):
        for x in range(4):
            for y in range(4):
                source, spot = ext_source(x, y, z, own, xlo, xhi, ylo, yhi, None, None)
                ref[x * 4 + y] = source[spot]


def load_own(own_ref, nf_ref, near_ref, ownpos_ref):
    for c in range(CELLS):
        nf_ref[c * SLOTS : (c + 1) * SLOTS, :] = own_ref[c, 0:SLOTS, :]
        line = line_of(own_ref, c, 3)
        for k, spot in enumerate(own_xyz(c)):
            moved = line[:, k * SLOTS : (k + 1) * SLOTS] + (spot + 1) * CUTOFF
            near_ref[k : k + 1, c * SLOTS : (c + 1) * SLOTS] = moved
    for half in range(2):
        lanes = slice(half * 128, half * 128 + 128)
        for k in range(3):
            ownpos_ref[k, lanes, :] = lane_to_rows(near_ref[k : k + 1, lanes])


def geometry_of(near_ref, ownpos_ref, cell, block, tile, own_pairs):
    lanes = slice(tile * 128, tile * 128 + 128)
    near = [near_ref[k : k + 1, lanes] for k in range(3)]
    start = pl.multiple_of(cell * SLOTS + block * 16, 16)
    own = [ownpos_ref[k, pl.ds(start, 16), :] for k in range(3)]
    return pair_geometry(near, own, start - tile * 128 if own_pairs else None)


def build_table(table_ref, geometry, tiles):
    for tile in range(tiles):
        lanes = slice(tile * 128, tile * 128 + 128)
        for block in range(2):
            inv, ux, uy, uz, first, cosine, env, denv = geometry(block, tile)
            radial = [(value * env).astype(BF16) for value in sine_series(first, cosine)]
            shape = [None] + [value.astype(BF16) for value in harmonics(ux, uy, uz)[1:]]
            for b in range(NB):
                for m in range(NM):
                    row = block * HALF + (b * NM + m) * 16
                    value = radial[b] if m == 0 else radial[b] * shape[m]
                    table_ref[row : row + 16, lanes] = value.astype(BF16)


def weigh(dens_ref, rw_ref, block, m):
    total = None
    for b in range(NB):
        row = block * HALF + (b * NM + m) * 16
        weight = rw_ref[DEG[m], b : b + 1, :]
        term = dens_ref[row : row + 16, :] * weight
        total = term if total is None else total + term
    return total


def spread(mom_ref, cell, rw_ref, dd_ref):
    for block in range(2):
        for m in range(NM):
            cot = mom_ref[cell, m, block * 16 : block * 16 + 16, :]
            for b in range(NB):
                row = block * HALF + (b * NM + m) * 16
                weight = rw_ref[DEG[m], b : b + 1, :]
                dd_ref[row : row + 16, :] = (cot * weight).astype(BF16)


def pairwise(terms):
    while len(terms) > 2:
        terms = [a + b for a, b in zip(terms[::2], terms[1::2])]
    return terms[0].astype(F32) + terms[1].astype(F32)


def pair_forces(geometry, dd_ref, nf_ref, dt_ref, width, near_out, fown_ref):
    pulls = [[None] * 3, [None] * 3]
    for chunk in range((width + 255) // 256):
        low = chunk * 256
        high = min(low + 256, width)
        slab = dt_ref.at[chunk % 2]
        slab[:, : high - low] = contract_last(dd_ref[...], nf_ref[low:high, :])
        for tile in range(low // 128, high // 128):
            inside = slice(tile * 128 - low, tile * 128 - low + 128)
            near_sum = [None] * 3
            for block in range(2):
                inv, ux, uy, uz, first, cosine, env, denv = geometry(block, tile)
                sines = [v.astype(BF16) for v in sine_series(first, cosine)]
                cosines = [v.astype(BF16) for v in cosine_series(cosine)]
                shape = harmonics(ux, uy, uz)
                pull = [None] * NM
                total_s = None
                total_c = None
                for m in range(NM):
                    ones, twos = [], []
                    for b in range(NB):
                        row = block * HALF + (b * NM + m) * 16
                        value = slab[row : row + 16, inside].astype(BF16)
                        ones.append(value * sines[b])
                        twos.append(value * cosines[b])
                    part_s, part_c = pairwise(ones), pairwise(twos)
                    pull[m] = part_s
                    if m == 0:
                        total_s, total_c = part_s, part_c
                    else:
                        total_s = total_s + part_s * shape[m]
                        total_c = total_c + part_c * shape[m]
                gx = ROOT3 * pull[1] + ROOT15 * (uy * pull[4] + uz * pull[7] + ux * pull[8])
                gy = ROOT3 * pull[2] + ROOT15 * (ux * pull[4] + uz * pull[5] - uy * pull[8])
                gz = (
                    ROOT3 * pull[3]
                    + ROOT15 * (uy * pull[5] + ux * pull[7])
                    + (3.0 * ROOT5) * uz * pull[6]
                )
                scale = env * inv
                turn = ux * gx + uy * gy + uz * gz
                wave = (math.pi / CUTOFF * NORM) * total_c
                along = denv * total_s + scale * (wave - total_s - turn)
                for k, (unit, side) in enumerate(((ux, gx), (uy, gy), (uz, gz))):
                    force = unit * along + scale * side
                    near_sum[k] = force if block == 0 else near_sum[k] + force
                    held = pulls[block][k]
                    pulls[block][k] = force if held is None else held + force
            near_out(tile, [jnp.sum(value, axis=0, keepdims=True) for value in near_sum])
    for k in range(3):
        for block in range(2):
            fown_ref[k * SLOTS + block * 16 : k * SLOTS + block * 16 + 16, :] = pulls[block][k]
    return jnp.sum(fown_ref[...].T, axis=0, keepdims=True)


def own_forward_kernel(first, own_ref, rw_ref, mom_ref, nf_ref, near_ref, ownpos_ref, table_ref, dens_ref):
    load_own(own_ref, nf_ref, near_ref, ownpos_ref)

    def step(pair, carry):
        for side in range(2):
            cell = first + pair * 2 + side

            def geometry(block, tile, cell=cell):
                return geometry_of(near_ref, ownpos_ref, cell, block, tile, True)

            build_table(table_ref.at[side], geometry, 2)
        for side in range(2):
            dens_ref[side] = jnp.dot(table_ref[side], nf_ref[...], preferred_element_type=F32)
        for side in range(2):
            at = pair * 2 + side
            for block in range(2):
                for m in range(NM):
                    rows = slice(block * 16, block * 16 + 16)
                    mom_ref[at, m, rows, :] = weigh(dens_ref.at[side], rw_ref, block, m)
        return carry

    lax.fori_loop(0, mom_ref.shape[0] // 2, step, 0)


def own_backward_kernel(
    first, count, own_ref, rw_ref, mom_ref, gown_ref, lines_ref,
    nf_ref, near_ref, ownpos_ref, table_ref, dd_ref, dt_ref, gnear_ref, fown_ref, gsum_ref,
):
    load_own(own_ref, nf_ref, near_ref, ownpos_ref)
    gsum_ref[...] = jnp.zeros_like(gsum_ref)
    gnear_ref[...] = jnp.zeros_like(gnear_ref)
    fown_ref[...] = jnp.zeros_like(fown_ref)
    lines_ref[...] = jnp.zeros_like(lines_ref)

    def near_out(tile, sums):
        for k in range(3):
            gnear_ref[k : k + 1, tile * 128 : tile * 128 + 128] += sums[k]

    def step(pair, carry):
        for side in range(2):
            cell = first + pair * 2 + side
            spread(mom_ref, cell, rw_ref, dd_ref.at[side])
        for side in range(2):
            cell = first + pair * 2 + side

            def geometry(block, tile, cell=cell):
                return geometry_of(near_ref, ownpos_ref, cell, block, tile, True)

            build_table(table_ref.at[side], geometry, 2)
            gsum_ref[...] += lax.dot_general(
                dd_ref[side], table_ref[side], (((0,), (0,)), ((), ())), preferred_element_type=F32
            )
            line = pair_forces(
                geometry, dd_ref.at[side], nf_ref, dt_ref.at[side], OWN, near_out, fown_ref.at[side]
            )
            lines_ref[pl.ds(cell, 1), :] = -line
        return carry

    lax.fori_loop(0, count // 2, step, 0)
    gown_ref[...] = gsum_ref[...].T
    for c in range(CELLS):
        for k in range(3):
            lanes = slice(k * SLOTS, (k + 1) * SLOTS)
            lines_ref[c : c + 1, lanes] += gnear_ref[k : k + 1, c * SLOTS : (c + 1) * SLOTS]


def ghost_kernel(
    parts, *refs
):
    counts_ref, edges_ref, own, xlo, xhi, ylo, yhi, zlo, zhi = refs[:9]
    refs = refs[1:]
    mom_in = refs[8 : 8 + parts]
    species_ref, rw_ref, mix_ref, skip_ref, readout_ref = refs[8 + parts : 13 + parts]
    new_ref, szlo, szhi, rest_ref, rlines_ref, cot_ref = refs[13 + parts : 19 + parts]
    (
        feat_ref, pos_ref, lines_ref, nf_ref, near_ref, ownnf_ref, ownnear_ref, ownpos_ref, kind_ref,
        table_ref, dens_ref, mom_ref, dd_ref, dt_ref, gnear_ref, fown_ref, gfeat_ref, gpos_ref, sline_ref, oline_ref,
    ) = refs[19 + parts :]
    load_own(own, ownnf_ref, ownnear_ref, ownpos_ref)
    for c in range(CELLS):
        sline_ref[0:1, c * SLOTS : (c + 1) * SLOTS] = species_ref[c : c + 1, :].astype(F32)
    for half in range(2):
        lanes = slice(half * 128, half * 128 + 128)
        kind_ref[lanes, :] = lane_to_rows(sline_ref[0:1, lanes])
    for x in range(4):
        for y in range(4):
            for z in range(4):
                source, spot = ext_source(x, y, z, own, xlo, xhi, ylo, yhi, zlo, zhi)
                cell = flat(x, y, z)
                feat_ref[cell] = source[spot, 0:SLOTS, :]
                lines_ref[cell : cell + 1, :] = line_of(source, spot, 3)
    index = lax.broadcasted_iota(jnp.int32, (64, SLOTS), 0)
    spots = (index >> 4, (index >> 2) & 3, index & 3)
    depth = spots[2]
    outside = ((depth == 0) & (edges_ref[0] > 0)) | ((depth == 3) & (edges_ref[1] > 0))
    for k in range(3):
        value = jnp.where(outside, SENTINEL, lines_ref[:, k * SLOTS : (k + 1) * SLOTS])
        pos_ref[k, :, 0:SLOTS] = value + spots[k].astype(F32) * CUTOFF
    spare = GWIDTH - GHOSTS * SLOTS
    near_ref[:, :, GHOSTS * SLOTS :] = jnp.full((2, 8, spare), 5000.0, F32)
    nf_ref[:, GHOSTS * SLOTS :, :] = jnp.zeros((2, spare, K), BF16)
    gnear_ref[...] = jnp.zeros_like(gnear_ref)
    gfeat_ref[...] = jnp.zeros_like(gfeat_ref)
    gpos_ref[...] = jnp.zeros_like(gpos_ref)
    fown_ref[...] = jnp.zeros_like(fown_ref)
    oline_ref[...] = jnp.zeros_like(oline_ref)

    def ghost_cell(cell, which):
        return flat(*(3 * at if side == 2 else side + 1 for side, at in zip(which, own_xyz(cell))))

    def load_ghosts(cell, side=0):
        for g, which in enumerate(GHOST_LIST):
            spot = ghost_cell(cell, which)
            nf_ref[side, g * SLOTS : (g + 1) * SLOTS, :] = feat_ref[spot]
            for k in range(3):
                near_ref[side, k : k + 1, g * SLOTS : (g + 1) * SLOTS] = pos_ref[k, pl.ds(spot, 1), 0:SLOTS]

    def geometry_at(cell, side=0):
        return lambda block, tile: geometry_of(near_ref.at[side], ownpos_ref, cell, block, tile, False)

    at = 0
    for held in mom_in:
        mom_ref[at : at + held.shape[0]] = held[...]
        at += held.shape[0]

    def forward(pair, carry):
        for side in range(2):
            load_ghosts(pair * 2 + side, side)
        for side in range(2):
            cell = pair * 2 + side
            build_table(table_ref.at[pair, side], geometry_at(cell, side), GWIDTH // 128)
        for side in range(2):
            dens_ref[side] = jnp.dot(table_ref[pair, side], nf_ref[side], preferred_element_type=F32)
        for side in range(2):
            cell = pair * 2 + side
            for block in range(2):
                for m in range(NM):
                    rows = slice(block * 16, block * 16 + 16)
                    mom_ref[cell, m, rows, :] += weigh(dens_ref.at[side], rw_ref, block, m)
        return carry

    lax.fori_loop(0, CELLS // 2, forward, 0)

    moments = [mom_ref[:, m].reshape(OWN, K) for m in range(NM)]
    product = moments[0]
    for m in range(1, NM):
        product = product + moments[m] * moments[m]
    own_feat = ownnf_ref[...]
    kinds = kind_ref[...]
    updated = jnp.dot(product.astype(BF16), mix_ref[...], preferred_element_type=F32)
    chosen = jnp.zeros((OWN, K), F32)
    for k in range(SPECIES):
        hot = kinds == float(k)
        masked = jnp.where(hot, own_feat.astype(F32), 0.0).astype(BF16)
        updated = updated + jnp.dot(masked, skip_ref[k], preferred_element_type=F32)
        chosen = jnp.where(hot, readout_ref[k : k + 1, :], chosen)
    slot = lax.broadcasted_iota(jnp.int32, (SLOTS, K), 0)
    alive = jnp.concatenate(
        [jnp.where(slot < counts_ref[own_xyz(c)], 1.0, 0.0) for c in range(CELLS)], axis=0
    )
    new_ref[...] = (updated * alive).astype(BF16)
    gate = 1.0 / (1.0 + jnp.exp(-updated))
    dupdated = alive * chosen * gate * (1.0 + updated * (1.0 - gate))
    dproduct = contract_last(dupdated.astype(BF16), mix_ref[...])
    dskip = jnp.zeros((OWN, K), F32)
    for k in range(SPECIES):
        masked = jnp.where(kinds == float(k), dupdated, 0.0).astype(BF16)
        dskip = dskip + contract_last(masked, skip_ref[k])
    for c in range(CELLS):
        x, y, z = own_xyz(c)
        gfeat_ref[flat(x + 1, y + 1, z + 1)] = dskip[c * SLOTS : (c + 1) * SLOTS, :]
    cot_ref[:, 0] = dproduct.reshape(CELLS, SLOTS, K)
    for m in range(1, NM):
        cot_ref[:, m] = (2.0 * moments[m] * dproduct).reshape(CELLS, SLOTS, K)

    def near_out(tile, sums):
        for k in range(3):
            gnear_ref[k : k + 1, tile * 128 : tile * 128 + 128] = sums[k]

    def backward(pair, carry):
        for side in range(2):
            cell = pair * 2 + side
            load_ghosts(cell, side)
            spread(cot_ref, cell, rw_ref, dd_ref.at[side])
        parts = []
        for side in range(2):
            cell = pair * 2 + side
            grads = lax.dot_general(
                dd_ref[side], table_ref[pair, side], (((0,), (0,)), ((), ())), preferred_element_type=F32
            ).T
            for g, which in enumerate(GHOST_LIST):
                gfeat_ref[ghost_cell(cell, which)] += grads[g * SLOTS : (g + 1) * SLOTS, :]
            line = pair_forces(
                geometry_at(cell, side), dd_ref.at[side], nf_ref.at[side], dt_ref, GWIDTH, near_out, fown_ref
            )
            oline_ref[pl.ds(cell, 1), :] = -line
            for g, which in enumerate(GHOST_LIST):
                spot = ghost_cell(cell, which)
                for k in range(3):
                    gpos_ref[k, pl.ds(spot, 1), 0:SLOTS] += gnear_ref[
                        k : k + 1, g * SLOTS : (g + 1) * SLOTS
                    ]
        return carry

    lax.fori_loop(0, CELLS // 2, backward, 0)

    for k in range(3):
        lines_ref[:, k * SLOTS : (k + 1) * SLOTS] = gpos_ref[k, :, 0:SLOTS]
    for c in range(CELLS):
        cell = flat(*(at + 1 for at in own_xyz(c)))
        lines_ref[cell : cell + 1, :] = oline_ref[c : c + 1, :]
    pieces = split_line(lines_ref[...], 2)
    for x in range(4):
        for y in range(4):
            for z in (1, 2):
                at, cell = (x * 4 + y) * 2 + z - 1, flat(x, y, z)
                rest_ref[at] = gfeat_ref[cell]
                rlines_ref[at : at + 1, :] = lines_ref[cell : cell + 1, :]
            for z, ref in ((0, szlo), (3, szhi)):
                at, cell = x * 4 + y, flat(x, y, z)
                ref[at, 0:SLOTS, :] = gfeat_ref[cell].astype(BF16)
                ref[at, SLOTS:ROW, :] = tail_of([piece[cell : cell + 1, :] for piece in pieces])


def gathered(x, y, z, rest_ref, rlines_ref, zs, ys, xs):
    at = (x * 4 + y) * 2 + z - 1
    feat = rest_ref[at]
    line = rlines_ref[at : at + 1, :]
    for faces, side, spot in (
        (zs, z, x * 4 + y),
        (ys, y, x * 2 + z - 1),
        (xs, x, (y - 1) * 2 + z - 1),
    ):
        if faces is not None:
            ref = faces[side - 1]
            feat = feat + ref[spot, 0:SLOTS, :].astype(F32)
            line = line + line_of(ref, spot, 2)
    return feat, line


def back_y_kernel(rest_ref, rlines_ref, zlo, zhi, lo_ref, hi_ref):
    for y, ref in ((0, lo_ref), (3, hi_ref)):
        for x in range(4):
            for z in (1, 2):
                feat, line = gathered(x, y, z, rest_ref, rlines_ref, (zlo, zhi), None, None)
                spot = x * 2 + z - 1
                ref[spot, 0:SLOTS, :] = feat.astype(BF16)
                ref[spot, SLOTS:ROW, :] = tail_of(split_line(line, 2))


def back_x_kernel(rest_ref, rlines_ref, zlo, zhi, ylo, yhi, lo_ref, hi_ref):
    for x, ref in ((0, lo_ref), (3, hi_ref)):
        for y in (1, 2):
            for z in (1, 2):
                feat, line = gathered(x, y, z, rest_ref, rlines_ref, (zlo, zhi), (ylo, yhi), None)
                spot = (y - 1) * 2 + z - 1
                ref[spot, 0:SLOTS, :] = feat.astype(BF16)
                ref[spot, SLOTS:ROW, :] = tail_of(split_line(line, 2))


def finish_kernel(parts, *refs):
    counts_ref, rest_ref, rlines_ref, zlo, zhi, ylo, yhi, xlo, xhi = refs[:9]
    gowns, lines = refs[9 : 9 + parts], refs[9 + parts : 9 + 2 * parts]
    grad_ref, force_ref = refs[9 + 2 * parts :]
    lane = lax.broadcasted_iota(jnp.int32, (1, SLOTS), 1)
    for c in range(CELLS):
        x, y, z = (at + 1 for at in own_xyz(c))
        feat, line = gathered(x, y, z, rest_ref, rlines_ref, (zlo, zhi), (ylo, yhi), (xlo, xhi))
        for gown, own_line in zip(gowns, lines):
            feat = feat + gown[c * SLOTS : (c + 1) * SLOTS, :]
            line = line + own_line[c : c + 1, :]
        grad_ref[c] = feat
        for k in range(3):
            x, y, z = own_xyz(c)
            force = jnp.where(lane < counts_ref[x, y, z], -line[:, k * SLOTS : (k + 1) * SLOTS], 0.0)
            force_ref[x, y, k, z : z + 1, :] = force


VMEM_SPEC = pl.BlockSpec(memory_space=pltpu.VMEM)
SMEM_SPEC = pl.BlockSpec(memory_space=pltpu.SMEM)


def call(kernel, name, shapes, args, scalars=0, scratch=(), limit=16, flops=0):
    out_shape = tuple(jax.ShapeDtypeStruct(shape, dtype) for shape, dtype in shapes)
    return pl.pallas_call(
        kernel,
        out_shape=out_shape,
        in_specs=[SMEM_SPEC] * scalars + [VMEM_SPEC] * (len(args) - scalars),
        out_specs=tuple(VMEM_SPEC for _ in shapes),
        scratch_shapes=list(scratch),
        compiler_params=pltpu.CompilerParams(vmem_limit_bytes=limit * 1024 * 1024),
        cost_estimate=pl.CostEstimate(flops=flops, bytes_accessed=1 << 20, transcendentals=0),
        name=name,
    )(*args)


def faces(cells):
    return [((cells, ROW, K), BF16)] * 2


def own_forward(own, rw, first, count):
    return call(
        partial(own_forward_kernel, first),
        "own_forward",
        [((count, NM, SLOTS, K), F32)],
        (own, rw),
        scratch=[
            pltpu.VMEM((OWN, K), BF16),
            pltpu.VMEM((8, OWN), F32),
            pltpu.VMEM((3, OWN, 128), F32),
            pltpu.VMEM((2, ROWS, OWN), BF16),
            pltpu.VMEM((2, ROWS, K), F32),
        ],
        flops=8 * count * ROWS * OWN * K,
    )[0]


def own_backward(own, rw, cot, first, count):
    return call(
        partial(own_backward_kernel, first, count),
        "own_backward",
        [((OWN, K), F32), ((CELLS, 128), F32)],
        (own, rw, cot),
        scratch=[
            pltpu.VMEM((OWN, K), BF16),
            pltpu.VMEM((8, OWN), F32),
            pltpu.VMEM((3, OWN, 128), F32),
            pltpu.VMEM((2, ROWS, OWN), BF16),
            pltpu.VMEM((2, ROWS, K), BF16),
            pltpu.VMEM((2, 1, ROWS, 256), F32),
            pltpu.VMEM((8, OWN), F32),
            pltpu.VMEM((2, 128, 128), F32),
            pltpu.VMEM((K, OWN), F32),
        ],
        flops=16 * count * ROWS * OWN * K,
    )


def ghost(counts, edges, payloads, moms, species, rw, mix, skip, readout):
    return call(
        partial(ghost_kernel, len(moms)),
        "ghost",
        [((OWN, K), BF16)]
        + faces(16)
        + [((32, SLOTS, K), F32), ((32, 128), F32), ((CELLS, NM, SLOTS, K), F32)],
        (counts, edges, *payloads, *moms, species, rw, mix, skip, readout),
        scalars=2,
        scratch=[
            pltpu.VMEM((64, SLOTS, K), BF16),
            pltpu.VMEM((3, 64, 128), F32),
            pltpu.VMEM((64, 128), F32),
            pltpu.VMEM((2, GWIDTH, K), BF16),
            pltpu.VMEM((2, 8, GWIDTH), F32),
            pltpu.VMEM((OWN, K), BF16),
            pltpu.VMEM((8, OWN), F32),
            pltpu.VMEM((3, OWN, 128), F32),
            pltpu.VMEM((OWN, 128), F32),
            pltpu.VMEM((CELLS // 2, 2, ROWS, GWIDTH), BF16),
            pltpu.VMEM((2, ROWS, K), F32),
            pltpu.VMEM((CELLS, NM, SLOTS, K), F32),
            pltpu.VMEM((2, ROWS, K), BF16),
            pltpu.VMEM((2, ROWS, 256), F32),
            pltpu.VMEM((8, GWIDTH), F32),
            pltpu.VMEM((128, 128), F32),
            pltpu.VMEM((64, SLOTS, K), F32),
            pltpu.VMEM((3, 64, 128), F32),
            pltpu.VMEM((8, OWN), F32),
            pltpu.VMEM((CELLS, 128), F32),
        ],
        limit=40,
        flops=16 * CELLS * ROWS * GWIDTH * K,
    )


def first_payloads(counts, features, positions):
    shapes = [((CELLS, ROW, K), BF16)] + faces(4)
    anywhere = pl.BlockSpec(memory_space=pl.ANY)

    def kernel(counts_in, feat_in, pos_in, *refs):
        counts_ref, feat_ref, pos_ref, line_ref, sems = refs[3:]
        copies = [
            pltpu.make_async_copy(source, target, sems.at[k])
            for k, (source, target) in enumerate(
                ((counts_in, counts_ref), (pos_in, pos_ref), (feat_in, feat_ref))
            )
        ]
        for copy in copies:
            copy.start()
        for copy in copies:
            copy.wait()
        pack_x_kernel(counts_ref, feat_ref, pos_ref, *refs[:3], line_ref)

    return pl.pallas_call(
        kernel,
        out_shape=tuple(jax.ShapeDtypeStruct(shape, dtype) for shape, dtype in shapes),
        in_specs=[anywhere] * 3,
        out_specs=(VMEM_SPEC,) * 3,
        scratch_shapes=[
            pltpu.VMEM(counts.shape, counts.dtype),
            pltpu.VMEM(features.shape, features.dtype),
            pltpu.VMEM(positions.shape, positions.dtype),
            pltpu.VMEM((CELLS, 128), F32),
            pltpu.SemaphoreType.DMA((3,)),
        ],
        compiler_params=pltpu.CompilerParams(vmem_limit_bytes=16 * 1024 * 1024),
        cost_estimate=pl.CostEstimate(flops=0, bytes_accessed=1 << 20, transcendentals=0),
        name="pack_x",
    )(counts, features, positions)


def moved(lo, hi, axis, ring):
    size = lax.axis_size(axis)
    up = [(i, (i + 1) % size) for i in range(size if ring else size - 1)]
    down = [(j, i) for i, j in up]
    return lax.ppermute(hi, axis, up), lax.ppermute(lo, axis, down)


FORWARD_PARTS = ((0, 2), (2, 2), (4, 4))
BACKWARD_PARTS = ((0, 4), (4, 2), (6, 2))


def after(values, done):
    return lax.optimization_barrier((values, done))[0]


def shards(features, positions, counts, species, radial_weight, mix_weight, skip_weight, readout):
    plane = lax.axis_index("gz")
    edges = jnp.stack([plane == 0, plane == lax.axis_size("gz") - 1]).astype(jnp.int32)
    rw = jnp.transpose(radial_weight, (1, 0, 2))
    own, xlo, xhi = first_payloads(
        counts, features.reshape(CELLS, SLOTS, K), jnp.transpose(positions, (0, 1, 3, 2, 4))
    )
    xs = moved(xlo, xhi, "gx", True)
    moms = [own_forward(own, rw, *FORWARD_PARTS[0])]
    xs = after(xs, moms[0])
    ylo, yhi = call(pack_y_kernel, "pack_y", faces(8), (own, *xs))
    ys = moved(ylo, yhi, "gy", True)
    moms.append(own_forward(after(own, ylo), rw, *FORWARD_PARTS[1]))
    ys = after(ys, moms[1])
    zlo, zhi = call(pack_z_kernel, "pack_z", faces(16), (own, *xs, *ys))
    zs = moved(zlo, zhi, "gz", False)
    moms.append(own_forward(after(own, zlo), rw, *FORWARD_PARTS[2]))
    new, bzlo, bzhi, rest, rlines, cot = ghost(
        counts,
        edges,
        (own, *xs, *ys, *zs),
        moms,
        species.reshape(CELLS, SLOTS),
        rw,
        mix_weight,
        skip_weight,
        readout,
    )
    zs = moved(bzlo, bzhi, "gz", False)
    backs = [own_backward(own, rw, cot, *BACKWARD_PARTS[0])]
    zs = after(zs, backs[0][0])
    bylo, byhi = call(back_y_kernel, "back_y", faces(8), (rest, rlines, *zs))
    ys = moved(bylo, byhi, "gy", True)
    backs.append(own_backward(after(own, bylo), rw, cot, *BACKWARD_PARTS[1]))
    ys = after(ys, backs[1][0])
    bxlo, bxhi = call(back_x_kernel, "back_x", faces(4), (rest, rlines, *zs, *ys))
    xs = moved(bxlo, bxhi, "gx", True)
    backs.append(own_backward(after(own, bxlo), rw, cot, *BACKWARD_PARTS[2]))
    grad, force = call(
        partial(finish_kernel, len(backs)),
        "finish",
        [((CELLS, SLOTS, K), F32), ((2, 2, 3, 2, SLOTS), F32)],
        (counts, rest, rlines, *zs, *ys, *xs, *(b[0] for b in backs), *(b[1] for b in backs)),
        scalars=1,
    )
    return (
        new.reshape(2, 2, 2, SLOTS, K),
        jnp.transpose(force, (0, 1, 3, 2, 4)),
        grad.reshape(2, 2, 2, SLOTS, K),
    )


def solution(mesh):
    cells = P("gx", "gy", "gz", None, None)
    return jax.shard_map(
        shards,
        mesh=mesh,
        in_specs=(cells, cells, P("gx", "gy", "gz"), P("gx", "gy", "gz", None), P(), P(), P(), P()),
        out_specs=(cells, cells, cells),
        check_vma=False,
    )
```

```python
from functools import partial
import math

import jax
import jax.numpy as jnp
from jax import lax
from jax.experimental import pallas as pl
from jax.experimental.pallas import tpu as pltpu
from jax.sharding import PartitionSpec as P

CUTOFF = 6.0
SENTINEL = 1000.0
SMALL = 1e-06
K = 128
NB = 8
NM = 9
SPECIES = 5
SLOTS = 32
CELLS = 8
DEG = (0, 1, 1, 1, 2, 2, 2, 2, 2)
OWN = CELLS * SLOTS
GHOSTS = 19
GWIDTH = 640
ROW = SLOTS + 16
HALF = NB * NM * 16
ROWS = 2 * HALF
F32 = jnp.float32
BF16 = jnp.bfloat16
ROOT3, ROOT5, ROOT15 = math.sqrt(3.0), math.sqrt(5.0), math.sqrt(15.0)
NORM = math.sqrt(2.0 / CUTOFF)
COS_FIT = (3.999999997, -3.739208102, 1.277990829, -0.2287452958, 0.02416752431)
SIN_FIT = (3.141592654, -5.167712765, 2.550163319, -0.5992521978, 0.08205040168, -0.00702838621)
GHOST_LIST = tuple(
    (a, b, c) for a in range(3) for b in range(3) for c in range(3) if 2 in (a, b, c)
)


def horner(coefs, y):
    acc = jnp.full_like(y, coefs[-1])
    for value in coefs[-2::-1]:
        acc = acc * y + value
    return acc


def pair_geometry(near, own, self_lane):
    dx, dy, dz = (near[k] - own[k] for k in range(3))
    inv = lax.rsqrt(dx * dx + dy * dy + dz * dz + SMALL)
    r2 = dx * dx + dy * dy + dz * dz + SMALL
    s = jnp.minimum(r2 * inv * (1.0 / CUTOFF), 1.0)
    ux, uy, uz = dx * inv, dy * inv, dz * inv
    t = 0.5 - s
    y = t * t
    first = (1.0 - s) * horner(COS_FIT, y) * (NORM / CUTOFF)
    cosine = t * horner(SIN_FIT, y)
    s2 = s * s
    s5 = s2 * s2 * s
    env = 1.0 - s5 * s * (28.0 - 48.0 * s + 21.0 * s2)
    away = 1.0 - s
    denv = s5 * (away * away) * (-168.0 / CUTOFF)
    if self_lane is not None:
        lane = lax.broadcasted_iota(jnp.int32, dx.shape, 1)
        row = lax.broadcasted_iota(jnp.int32, dx.shape, 0)
        same = lane == row + self_lane
        env = jnp.where(same, 0.0, env)
        denv = jnp.where(same, 0.0, denv)
    return inv, ux, uy, uz, first, cosine, env, denv


def sine_series(first, cosine):
    twice = cosine + cosine
    out = [first, twice * first]
    for _ in range(NB - 2):
        out.append(twice * out[-1] - out[-2])
    return out


def cosine_series(cosine):
    twice = cosine + cosine
    out = [cosine, twice * cosine - 1.0]
    for _ in range(NB - 2):
        out.append(twice * out[-1] - out[-2])
    return [float(b + 1) * value for b, value in enumerate(out)]


def harmonics(ux, uy, uz):
    return [
        None,
        ROOT3 * ux,
        ROOT3 * uy,
        ROOT3 * uz,
        ROOT15 * ux * uy,
        ROOT15 * uy * uz,
        0.5 * ROOT5 * (3.0 * uz * uz - 1.0),
        ROOT15 * ux * uz,
        0.5 * ROOT15 * (ux * ux - uy * uy),
    ]


def lane_to_rows(line):
    return jnp.broadcast_to(line, (128, 128)).T


def contract_last(a, b):
    return lax.dot_general(a, b, (((1,), (1,)), ((), ())), preferred_element_type=F32)


def flat(x, y, z):
    return x * 16 + y * 4 + z


def own_xyz(cell):
    return cell // 4, (cell // 2) % 2, cell % 2


def tail_of(rows):
    index = lax.broadcasted_iota(jnp.int32, (16, 128), 0)
    tail = jnp.zeros((16, 128), F32)
    for k, line in enumerate(rows):
        tail = jnp.where(index == k, jnp.broadcast_to(line, (16, 128)), tail)
    return tail.astype(BF16)


def split_line(line, pieces):
    out = []
    for _ in range(pieces):
        part = line.astype(BF16).astype(F32)
        out.append(part)
        line = line - part
    return out


def line_of(ref, cell, pieces):
    tail = ref[cell, SLOTS:ROW, :].astype(F32)
    line = tail[0:1, :]
    for k in range(1, pieces):
        line = line + tail[k : k + 1, :]
    return line


def ext_source(x, y, z, own, xlo, xhi, ylo, yhi, zlo, zhi):
    if z in (0, 3):
        return (zlo if z == 0 else zhi), x * 4 + y
    if y in (0, 3):
        return (ylo if y == 0 else yhi), x * 2 + z - 1
    if x in (0, 3):
        return (xlo if x == 0 else xhi), (y - 1) * 2 + z - 1
    return own, (x - 1) * 4 + (y - 1) * 2 + z - 1


def pack_x_kernel(counts_ref, feat_ref, pos_ref, own_ref, xlo_ref, xhi_ref, line_ref):
    lane = lax.broadcasted_iota(jnp.int32, (1, SLOTS), 1)
    line_ref[...] = jnp.zeros_like(line_ref)
    for c in range(CELLS):
        for k in range(3):
            x, y, z = own_xyz(c)
            value = pos_ref[x, y, k, z : z + 1, :]
            value = jnp.where(lane < counts_ref[x, y : y + 1, z : z + 1], value, SENTINEL)
            line_ref[c : c + 1, k * SLOTS : (k + 1) * SLOTS] = value
    pieces = split_line(line_ref[...], 3)
    for c in range(CELLS):
        tail = tail_of([piece[c : c + 1, :] for piece in pieces])
        feat = feat_ref[c]
        for ref, spot in ((own_ref, c), ((xlo_ref, xhi_ref)[c // 4], c % 4)):
            ref[spot, 0:SLOTS, :] = feat
            ref[spot, SLOTS:ROW, :] = tail


def pack_y_kernel(own, xlo, xhi, lo_ref, hi_ref):
    for y, ref in ((1, lo_ref), (2, hi_ref)):
        for x in range(4):
            for z in (1, 2):
                source, spot = ext_source(x, y, z, own, xlo, xhi, None, None, None, None)
                ref[x * 2 + z - 1] = source[spot]


def pack_z_kernel(own, xlo, xhi, ylo, yhi, lo_ref, hi_ref):
    for z, ref in ((1, lo_ref), (2, hi_ref)):
        for x in range(4):
            for y in range(4):
                source, spot = ext_source(x, y, z, own, xlo, xhi, ylo, yhi, None, None)
                ref[x * 4 + y] = source[spot]


def load_own(own_ref, nf_ref, near_ref, ownpos_ref):
    for c in range(CELLS):
        nf_ref[c * SLOTS : (c + 1) * SLOTS, :] = own_ref[c, 0:SLOTS, :]
        line = line_of(own_ref, c, 3)
        for k, spot in enumerate(own_xyz(c)):
            moved = line[:, k * SLOTS : (k + 1) * SLOTS] + (spot + 1) * CUTOFF
            near_ref[k : k + 1, c * SLOTS : (c + 1) * SLOTS] = moved
    for half in range(2):
        lanes = slice(half * 128, half * 128 + 128)
        for k in range(3):
            ownpos_ref[k, lanes, :] = lane_to_rows(near_ref[k : k + 1, lanes])


def geometry_of(near_ref, ownpos_ref, cell, block, tile, own_pairs):
    lanes = slice(tile * 128, tile * 128 + 128)
    near = [near_ref[k : k + 1, lanes] for k in range(3)]
    start = pl.multiple_of(cell * SLOTS + block * 16, 16)
    own = [ownpos_ref[k, pl.ds(start, 16), :] for k in range(3)]
    return pair_geometry(near, own, start - tile * 128 if own_pairs else None)


def build_table(table_ref, geometry, tiles):
    for tile in range(tiles):
        lanes = slice(tile * 128, tile * 128 + 128)
        for block in range(2):
            inv, ux, uy, uz, first, cosine, env, denv = geometry(block, tile)
            radial = [(value * env).astype(BF16) for value in sine_series(first, cosine)]
            shape = [None] + [value.astype(BF16) for value in harmonics(ux, uy, uz)[1:]]
            for b in range(NB):
                for m in range(NM):
                    row = block * HALF + (b * NM + m) * 16
                    value = radial[b] if m == 0 else radial[b] * shape[m]
                    table_ref[row : row + 16, lanes] = value.astype(BF16)


def weigh(dens_ref, rw_ref, block, m):
    total = None
    for b in range(NB):
        row = block * HALF + (b * NM + m) * 16
        weight = rw_ref[DEG[m], b : b + 1, :]
        term = dens_ref[row : row + 16, :] * weight
        total = term if total is None else total + term
    return total


def spread(mom_ref, cell, rw_ref, dd_ref):
    for block in range(2):
        for m in range(NM):
            cot = mom_ref[cell, m, block * 16 : block * 16 + 16, :]
            for b in range(NB):
                row = block * HALF + (b * NM + m) * 16
                weight = rw_ref[DEG[m], b : b + 1, :]
                dd_ref[row : row + 16, :] = (cot * weight).astype(BF16)


def pairwise(terms):
    while len(terms) > 2:
        terms = [a + b for a, b in zip(terms[::2], terms[1::2])]
    return terms[0].astype(F32) + terms[1].astype(F32)


def pair_forces(geometry, dd_ref, nf_ref, dt_ref, width, near_out, fown_ref):
    pulls = [[None] * 3, [None] * 3]
    for chunk in range((width + 255) // 256):
        low = chunk * 256
        high = min(low + 256, width)
        slab = dt_ref.at[chunk % 2]
        slab[:, : high - low] = contract_last(dd_ref[...], nf_ref[low:high, :])
        for tile in range(low // 128, high // 128):
            inside = slice(tile * 128 - low, tile * 128 - low + 128)
            near_sum = [None] * 3
            for block in range(2):
                inv, ux, uy, uz, first, cosine, env, denv = geometry(block, tile)
                sines = [v.astype(BF16) for v in sine_series(first, cosine)]
                cosines = [v.astype(BF16) for v in cosine_series(cosine)]
                shape = harmonics(ux, uy, uz)
                pull = [None] * NM
                total_s = None
                total_c = None
                for m in range(NM):
                    ones, twos = [], []
                    for b in range(NB):
                        row = block * HALF + (b * NM + m) * 16
                        value = slab[row : row + 16, inside].astype(BF16)
                        ones.append(value * sines[b])
                        twos.append(value * cosines[b])
                    part_s, part_c = pairwise(ones), pairwise(twos)
                    pull[m] = part_s
                    if m == 0:
                        total_s, total_c = part_s, part_c
                    else:
                        total_s = total_s + part_s * shape[m]
                        total_c = total_c + part_c * shape[m]
                gx = ROOT3 * pull[1] + ROOT15 * (uy * pull[4] + uz * pull[7] + ux * pull[8])
                gy = ROOT3 * pull[2] + ROOT15 * (ux * pull[4] + uz * pull[5] - uy * pull[8])
                gz = (
                    ROOT3 * pull[3]
                    + ROOT15 * (uy * pull[5] + ux * pull[7])
                    + (3.0 * ROOT5) * uz * pull[6]
                )
                scale = env * inv
                turn = ux * gx + uy * gy + uz * gz
                wave = (math.pi / CUTOFF * NORM) * total_c
                along = denv * total_s + scale * (wave - total_s - turn)
                for k, (unit, side) in enumerate(((ux, gx), (uy, gy), (uz, gz))):
                    force = unit * along + scale * side
                    near_sum[k] = force if block == 0 else near_sum[k] + force
                    held = pulls[block][k]
                    pulls[block][k] = force if held is None else held + force
            near_out(tile, [jnp.sum(value, axis=0, keepdims=True) for value in near_sum])
    for k in range(3):
        for block in range(2):
            fown_ref[k * SLOTS + block * 16 : k * SLOTS + block * 16 + 16, :] = pulls[block][k]
    return jnp.sum(fown_ref[...].T, axis=0, keepdims=True)


def own_forward_kernel(first, own_ref, rw_ref, mom_ref, nf_ref, near_ref, ownpos_ref, table_ref, dens_ref):
    load_own(own_ref, nf_ref, near_ref, ownpos_ref)

    def step(pair, carry):
        for side in range(2):
            cell = first + pair * 2 + side

            def geometry(block, tile, cell=cell):
                return geometry_of(near_ref, ownpos_ref, cell, block, tile, True)

            build_table(table_ref.at[side], geometry, 2)
        for side in range(2):
            dens_ref[side] = jnp.dot(table_ref[side], nf_ref[...], preferred_element_type=F32)
        for side in range(2):
            at = pair * 2 + side
            for block in range(2):
                for m in range(NM):
                    rows = slice(block * 16, block * 16 + 16)
                    mom_ref[at, m, rows, :] = weigh(dens_ref.at[side], rw_ref, block, m)
        return carry

    lax.fori_loop(0, mom_ref.shape[0] // 2, step, 0)


def own_backward_kernel(
    first, count, own_ref, rw_ref, mom_ref, gown_ref, lines_ref,
    nf_ref, near_ref, ownpos_ref, table_ref, dd_ref, dt_ref, gnear_ref, fown_ref, gsum_ref,
):
    load_own(own_ref, nf_ref, near_ref, ownpos_ref)
    gsum_ref[...] = jnp.zeros_like(gsum_ref)
    gnear_ref[...] = jnp.zeros_like(gnear_ref)
    fown_ref[...] = jnp.zeros_like(fown_ref)
    lines_ref[...] = jnp.zeros_like(lines_ref)

    def near_out(tile, sums):
        for k in range(3):
            gnear_ref[k : k + 1, tile * 128 : tile * 128 + 128] += sums[k]

    def step(pair, carry):
        for side in range(2):
            cell = first + pair * 2 + side
            spread(mom_ref, cell, rw_ref, dd_ref.at[side])
        for side in range(2):
            cell = first + pair * 2 + side

            def geometry(block, tile, cell=cell):
                return geometry_of(near_ref, ownpos_ref, cell, block, tile, True)

            build_table(table_ref.at[side], geometry, 2)
            gsum_ref[...] += lax.dot_general(
                dd_ref[side], table_ref[side], (((0,), (0,)), ((), ())), preferred_element_type=F32
            )
            line = pair_forces(
                geometry, dd_ref.at[side], nf_ref, dt_ref.at[side], OWN, near_out, fown_ref.at[side]
            )
            lines_ref[pl.ds(cell, 1), :] = -line
        return carry

    lax.fori_loop(0, count // 2, step, 0)
    gown_ref[...] = gsum_ref[...].T
    for c in range(CELLS):
        for k in range(3):
            lanes = slice(k * SLOTS, (k + 1) * SLOTS)
            lines_ref[c : c + 1, lanes] += gnear_ref[k : k + 1, c * SLOTS : (c + 1) * SLOTS]


def ghost_kernel(
    parts, *refs
):
    counts_ref, edges_ref, own, xlo, xhi, ylo, yhi, zlo, zhi = refs[:9]
    refs = refs[1:]
    mom_in = refs[8 : 8 + parts]
    species_ref, rw_ref, mix_ref, skip_ref, readout_ref = refs[8 + parts : 13 + parts]
    new_ref, szlo, szhi, rest_ref, rlines_ref, cot_ref = refs[13 + parts : 19 + parts]
    (
        feat_ref, pos_ref, lines_ref, nf_ref, near_ref, ownnf_ref, ownnear_ref, ownpos_ref, kind_ref,
        table_ref, dens_ref, mom_ref, dd_ref, dt_ref, gnear_ref, fown_ref, gfeat_ref, gpos_ref, sline_ref, oline_ref,
    ) = refs[19 + parts :]
    load_own(own, ownnf_ref, ownnear_ref, ownpos_ref)
    for c in range(CELLS):
        sline_ref[0:1, c * SLOTS : (c + 1) * SLOTS] = species_ref[c : c + 1, :].astype(F32)
    for half in range(2):
        lanes = slice(half * 128, half * 128 + 128)
        kind_ref[lanes, :] = lane_to_rows(sline_ref[0:1, lanes])
    for x in range(4):
        for y in range(4):
            for z in range(4):
                source, spot = ext_source(x, y, z, own, xlo, xhi, ylo, yhi, zlo, zhi)
                cell = flat(x, y, z)
                feat_ref[cell] = source[spot, 0:SLOTS, :]
                lines_ref[cell : cell + 1, :] = line_of(source, spot, 3)
    index = lax.broadcasted_iota(jnp.int32, (64, SLOTS), 0)
    spots = (index >> 4, (index >> 2) & 3, index & 3)
    depth = spots[2]
    outside = ((depth == 0) & (edges_ref[0] > 0)) | ((depth == 3) & (edges_ref[1] > 0))
    for k in range(3):
        value = jnp.where(outside, SENTINEL, lines_ref[:, k * SLOTS : (k + 1) * SLOTS])
        pos_ref[k, :, 0:SLOTS] = value + spots[k].astype(F32) * CUTOFF
    spare = GWIDTH - GHOSTS * SLOTS
    near_ref[:, :, GHOSTS * SLOTS :] = jnp.full((2, 8, spare), 5000.0, F32)
    nf_ref[:, GHOSTS * SLOTS :, :] = jnp.zeros((2, spare, K), BF16)
    gnear_ref[...] = jnp.zeros_like(gnear_ref)
    gfeat_ref[...] = jnp.zeros_like(gfeat_ref)
    gpos_ref[...] = jnp.zeros_like(gpos_ref)
    fown_ref[...] = jnp.zeros_like(fown_ref)
    oline_ref[...] = jnp.zeros_like(oline_ref)

    def ghost_cell(cell, which):
        return flat(*(3 * at if side == 2 else side + 1 for side, at in zip(which, own_xyz(cell))))

    def load_ghosts(cell, side=0):
        for g, which in enumerate(GHOST_LIST):
            spot = ghost_cell(cell, which)
            nf_ref[side, g * SLOTS : (g + 1) * SLOTS, :] = feat_ref[spot]
            for k in range(3):
                near_ref[side, k : k + 1, g * SLOTS : (g + 1) * SLOTS] = pos_ref[k, pl.ds(spot, 1), 0:SLOTS]

    def geometry_at(cell, side=0):
        return lambda block, tile: geometry_of(near_ref.at[side], ownpos_ref, cell, block, tile, False)

    at = 0
    for held in mom_in:
        mom_ref[at : at + held.shape[0]] = held[...]
        at += held.shape[0]

    def forward(pair, carry):
        for side in range(2):
            load_ghosts(pair * 2 + side, side)
        for side in range(2):
            cell = pair * 2 + side
            build_table(table_ref.at[pair, side], geometry_at(cell, side), GWIDTH // 128)
        for side in range(2):
            dens_ref[side] = jnp.dot(table_ref[pair, side], nf_ref[side], preferred_element_type=F32)
        for side in range(2):
            cell = pair * 2 + side
            for block in range(2):
                for m in range(NM):
                    rows = slice(block * 16, block * 16 + 16)
                    mom_ref[cell, m, rows, :] += weigh(dens_ref.at[side], rw_ref, block, m)
        return carry

    lax.fori_loop(0, CELLS // 2, forward, 0)

    moments = [mom_ref[:, m].reshape(OWN, K) for m in range(NM)]
    product = moments[0]
    for m in range(1, NM):
        product = product + moments[m] * moments[m]
    own_feat = ownnf_ref[...]
    kinds = kind_ref[...]
    updated = jnp.dot(product.astype(BF16), mix_ref[...], preferred_element_type=F32)
    chosen = jnp.zeros((OWN, K), F32)
    for k in range(SPECIES):
        hot = kinds == float(k)
        masked = jnp.where(hot, own_feat.astype(F32), 0.0).astype(BF16)
        updated = updated + jnp.dot(masked, skip_ref[k], preferred_element_type=F32)
        chosen = jnp.where(hot, readout_ref[k : k + 1, :], chosen)
    slot = lax.broadcasted_iota(jnp.int32, (SLOTS, K), 0)
    alive = jnp.concatenate(
        [jnp.where(slot < counts_ref[own_xyz(c)], 1.0, 0.0) for c in range(CELLS)], axis=0
    )
    new_ref[...] = (updated * alive).astype(BF16)
    gate = 1.0 / (1.0 + jnp.exp(-updated))
    dupdated = alive * chosen * gate * (1.0 + updated * (1.0 - gate))
    dproduct = contract_last(dupdated.astype(BF16), mix_ref[...])
    dskip = jnp.zeros((OWN, K), F32)
    for k in range(SPECIES):
        masked = jnp.where(kinds == float(k), dupdated, 0.0).astype(BF16)
        dskip = dskip + contract_last(masked, skip_ref[k])
    for c in range(CELLS):
        x, y, z = own_xyz(c)
        gfeat_ref[flat(x + 1, y + 1, z + 1)] = dskip[c * SLOTS : (c + 1) * SLOTS, :]
    cot_ref[:, 0] = dproduct.reshape(CELLS, SLOTS, K)
    for m in range(1, NM):
        cot_ref[:, m] = (2.0 * moments[m] * dproduct).reshape(CELLS, SLOTS, K)

    def near_out(tile, sums):
        for k in range(3):
            gnear_ref[k : k + 1, tile * 128 : tile * 128 + 128] = sums[k]

    def backward(pair, carry):
        for side in range(2):
            cell = pair * 2 + side
            load_ghosts(cell, side)
            spread(cot_ref, cell, rw_ref, dd_ref.at[side])
        parts = []
        for side in range(2):
            cell = pair * 2 + side
            grads = lax.dot_general(
                dd_ref[side], table_ref[pair, side], (((0,), (0,)), ((), ())), preferred_element_type=F32
            ).T
            for g, which in enumerate(GHOST_LIST):
                gfeat_ref[ghost_cell(cell, which)] += grads[g * SLOTS : (g + 1) * SLOTS, :]
            line = pair_forces(
                geometry_at(cell, side), dd_ref.at[side], nf_ref.at[side], dt_ref, GWIDTH, near_out, fown_ref
            )
            oline_ref[pl.ds(cell, 1), :] = -line
            for g, which in enumerate(GHOST_LIST):
                spot = ghost_cell(cell, which)
                for k in range(3):
                    gpos_ref[k, pl.ds(spot, 1), 0:SLOTS] += gnear_ref[
                        k : k + 1, g * SLOTS : (g + 1) * SLOTS
                    ]
        return carry

    lax.fori_loop(0, CELLS // 2, backward, 0)

    for k in range(3):
        lines_ref[:, k * SLOTS : (k + 1) * SLOTS] = gpos_ref[k, :, 0:SLOTS]
    for c in range(CELLS):
        cell = flat(*(at + 1 for at in own_xyz(c)))
        lines_ref[cell : cell + 1, :] = oline_ref[c : c + 1, :]
    pieces = split_line(lines_ref[...], 2)
    for x in range(4):
        for y in range(4):
            for z in (1, 2):
                at, cell = (x * 4 + y) * 2 + z - 1, flat(x, y, z)
                rest_ref[at] = gfeat_ref[cell]
                rlines_ref[at : at + 1, :] = lines_ref[cell : cell + 1, :]
            for z, ref in ((0, szlo), (3, szhi)):
                at, cell = x * 4 + y, flat(x, y, z)
                ref[at, 0:SLOTS, :] = gfeat_ref[cell].astype(BF16)
                ref[at, SLOTS:ROW, :] = tail_of([piece[cell : cell + 1, :] for piece in pieces])


def gathered(x, y, z, rest_ref, rlines_ref, zs, ys, xs):
    at = (x * 4 + y) * 2 + z - 1
    feat = rest_ref[at]
    line = rlines_ref[at : at + 1, :]
    for faces, side, spot in (
        (zs, z, x * 4 + y),
        (ys, y, x * 2 + z - 1),
        (xs, x, (y - 1) * 2 + z - 1),
    ):
        if faces is not None:
            ref = faces[side - 1]
            feat = feat + ref[spot, 0:SLOTS, :].astype(F32)
            line = line + line_of(ref, spot, 2)
    return feat, line


def back_y_kernel(rest_ref, rlines_ref, zlo, zhi, lo_ref, hi_ref):
    for y, ref in ((0, lo_ref), (3, hi_ref)):
        for x in range(4):
            for z in (1, 2):
                feat, line = gathered(x, y, z, rest_ref, rlines_ref, (zlo, zhi), None, None)
                spot = x * 2 + z - 1
                ref[spot, 0:SLOTS, :] = feat.astype(BF16)
                ref[spot, SLOTS:ROW, :] = tail_of(split_line(line, 2))


def back_x_kernel(rest_ref, rlines_ref, zlo, zhi, ylo, yhi, lo_ref, hi_ref):
    for x, ref in ((0, lo_ref), (3, hi_ref)):
        for y in (1, 2):
            for z in (1, 2):
                feat, line = gathered(x, y, z, rest_ref, rlines_ref, (zlo, zhi), (ylo, yhi), None)
                spot = (y - 1) * 2 + z - 1
                ref[spot, 0:SLOTS, :] = feat.astype(BF16)
                ref[spot, SLOTS:ROW, :] = tail_of(split_line(line, 2))


def finish_kernel(parts, *refs):
    counts_ref, rest_ref, rlines_ref, zlo, zhi, ylo, yhi, xlo, xhi = refs[:9]
    gowns, lines = refs[9 : 9 + parts], refs[9 + parts : 9 + 2 * parts]
    grad_ref, force_ref = refs[9 + 2 * parts :]
    lane = lax.broadcasted_iota(jnp.int32, (1, SLOTS), 1)
    for c in range(CELLS):
        x, y, z = (at + 1 for at in own_xyz(c))
        feat, line = gathered(x, y, z, rest_ref, rlines_ref, (zlo, zhi), (ylo, yhi), (xlo, xhi))
        for gown, own_line in zip(gowns, lines):
            feat = feat + gown[c * SLOTS : (c + 1) * SLOTS, :]
            line = line + own_line[c : c + 1, :]
        grad_ref[c] = feat
        for k in range(3):
            x, y, z = own_xyz(c)
            force = jnp.where(lane < counts_ref[x, y, z], -line[:, k * SLOTS : (k + 1) * SLOTS], 0.0)
            force_ref[x, y, k, z : z + 1, :] = force


VMEM_SPEC = pl.BlockSpec(memory_space=pltpu.VMEM)
SMEM_SPEC = pl.BlockSpec(memory_space=pltpu.SMEM)


def call(kernel, name, shapes, args, scalars=0, scratch=(), limit=16, flops=0):
    out_shape = tuple(jax.ShapeDtypeStruct(shape, dtype) for shape, dtype in shapes)
    return pl.pallas_call(
        kernel,
        out_shape=out_shape,
        in_specs=[SMEM_SPEC] * scalars + [VMEM_SPEC] * (len(args) - scalars),
        out_specs=tuple(VMEM_SPEC for _ in shapes),
        scratch_shapes=list(scratch),
        compiler_params=pltpu.CompilerParams(vmem_limit_bytes=limit * 1024 * 1024),
        cost_estimate=pl.CostEstimate(flops=flops, bytes_accessed=1 << 20, transcendentals=0),
        name=name,
    )(*args)


def faces(cells):
    return [((cells, ROW, K), BF16)] * 2


def own_forward(own, rw, first, count):
    return call(
        partial(own_forward_kernel, first),
        "own_forward",
        [((count, NM, SLOTS, K), F32)],
        (own, rw),
        scratch=[
            pltpu.VMEM((OWN, K), BF16),
            pltpu.VMEM((8, OWN), F32),
            pltpu.VMEM((3, OWN, 128), F32),
            pltpu.VMEM((2, ROWS, OWN), BF16),
            pltpu.VMEM((2, ROWS, K), F32),
        ],
        flops=8 * count * ROWS * OWN * K,
    )[0]


def own_backward(own, rw, cot, first, count):
    return call(
        partial(own_backward_kernel, first, count),
        "own_backward",
        [((OWN, K), F32), ((CELLS, 128), F32)],
        (own, rw, cot),
        scratch=[
            pltpu.VMEM((OWN, K), BF16),
            pltpu.VMEM((8, OWN), F32),
            pltpu.VMEM((3, OWN, 128), F32),
            pltpu.VMEM((2, ROWS, OWN), BF16),
            pltpu.VMEM((2, ROWS, K), BF16),
            pltpu.VMEM((2, 1, ROWS, 256), F32),
            pltpu.VMEM((8, OWN), F32),
            pltpu.VMEM((2, 128, 128), F32),
            pltpu.VMEM((K, OWN), F32),
        ],
        flops=16 * count * ROWS * OWN * K,
    )


def ghost(counts, edges, payloads, moms, species, rw, mix, skip, readout):
    return call(
        partial(ghost_kernel, len(moms)),
        "ghost",
        [((OWN, K), BF16)]
        + faces(16)
        + [((32, SLOTS, K), F32), ((32, 128), F32), ((CELLS, NM, SLOTS, K), F32)],
        (counts, edges, *payloads, *moms, species, rw, mix, skip, readout),
        scalars=2,
        scratch=[
            pltpu.VMEM((64, SLOTS, K), BF16),
            pltpu.VMEM((3, 64, 128), F32),
            pltpu.VMEM((64, 128), F32),
            pltpu.VMEM((2, GWIDTH, K), BF16),
            pltpu.VMEM((2, 8, GWIDTH), F32),
            pltpu.VMEM((OWN, K), BF16),
            pltpu.VMEM((8, OWN), F32),
            pltpu.VMEM((3, OWN, 128), F32),
            pltpu.VMEM((OWN, 128), F32),
            pltpu.VMEM((CELLS // 2, 2, ROWS, GWIDTH), BF16),
            pltpu.VMEM((2, ROWS, K), F32),
            pltpu.VMEM((CELLS, NM, SLOTS, K), F32),
            pltpu.VMEM((2, ROWS, K), BF16),
            pltpu.VMEM((2, ROWS, 256), F32),
            pltpu.VMEM((8, GWIDTH), F32),
            pltpu.VMEM((128, 128), F32),
            pltpu.VMEM((64, SLOTS, K), F32),
            pltpu.VMEM((3, 64, 128), F32),
            pltpu.VMEM((8, OWN), F32),
            pltpu.VMEM((CELLS, 128), F32),
        ],
        limit=40,
        flops=16 * CELLS * ROWS * GWIDTH * K,
    )


def first_payloads(counts, features, positions):
    shapes = [((CELLS, ROW, K), BF16)] + faces(4)
    anywhere = pl.BlockSpec(memory_space=pl.ANY)

    def kernel(counts_in, feat_in, pos_in, *refs):
        counts_ref, feat_ref, pos_ref, line_ref, sems = refs[3:]
        copies = [
            pltpu.make_async_copy(source, target, sems.at[k])
            for k, (source, target) in enumerate(
                ((counts_in, counts_ref), (pos_in, pos_ref), (feat_in, feat_ref))
            )
        ]
        for copy in copies:
            copy.start()
        for copy in copies:
            copy.wait()
        pack_x_kernel(counts_ref, feat_ref, pos_ref, *refs[:3], line_ref)

    return pl.pallas_call(
        kernel,
        out_shape=tuple(jax.ShapeDtypeStruct(shape, dtype) for shape, dtype in shapes),
        in_specs=[anywhere] * 3,
        out_specs=(VMEM_SPEC,) * 3,
        scratch_shapes=[
            pltpu.VMEM(counts.shape, counts.dtype),
            pltpu.VMEM(features.shape, features.dtype),
            pltpu.VMEM(positions.shape, positions.dtype),
            pltpu.VMEM((CELLS, 128), F32),
            pltpu.SemaphoreType.DMA((3,)),
        ],
        compiler_params=pltpu.CompilerParams(vmem_limit_bytes=60 * 1024 * 1024),
        cost_estimate=pl.CostEstimate(flops=0, bytes_accessed=1 << 20, transcendentals=0),
        name="pack_x",
    )(counts, features, positions)


def moved(lo, hi, axis, ring):
    size = lax.axis_size(axis)
    up = [(i, (i + 1) % size) for i in range(size if ring else size - 1)]
    down = [(j, i) for i, j in up]
    return lax.ppermute(hi, axis, up), lax.ppermute(lo, axis, down)


FORWARD_PARTS = ((0, 2), (2, 2), (4, 4))
BACKWARD_PARTS = ((0, 4), (4, 2), (6, 2))


def after(values, done):
    return lax.optimization_barrier((values, done))[0]


def shards(features, positions, counts, species, radial_weight, mix_weight, skip_weight, readout):
    plane = lax.axis_index("gz")
    edges = jnp.stack([plane == 0, plane == lax.axis_size("gz") - 1]).astype(jnp.int32)
    rw = jnp.transpose(radial_weight, (1, 0, 2))
    own, xlo, xhi = first_payloads(
        counts, features.reshape(CELLS, SLOTS, K), jnp.transpose(positions, (0, 1, 3, 2, 4))
    )
    xs = moved(xlo, xhi, "gx", True)
    moms = [own_forward(own, rw, *FORWARD_PARTS[0])]
    xs = after(xs, moms[0])
    ylo, yhi = call(pack_y_kernel, "pack_y", faces(8), (own, *xs))
    ys = moved(ylo, yhi, "gy", True)
    moms.append(own_forward(after(own, ylo), rw, *FORWARD_PARTS[1]))
    ys = after(ys, moms[1])
    zlo, zhi = call(pack_z_kernel, "pack_z", faces(16), (own, *xs, *ys))
    zs = moved(zlo, zhi, "gz", False)
    moms.append(own_forward(after(own, zlo), rw, *FORWARD_PARTS[2]))
    new, bzlo, bzhi, rest, rlines, cot = ghost(
        counts,
        edges,
        (own, *xs, *ys, *zs),
        moms,
        species.reshape(CELLS, SLOTS),
        rw,
        mix_weight,
        skip_weight,
        readout,
    )
    zs = moved(bzlo, bzhi, "gz", False)
    backs = [own_backward(own, rw, cot, *BACKWARD_PARTS[0])]
    zs = after(zs, backs[0][0])
    bylo, byhi = call(back_y_kernel, "back_y", faces(8), (rest, rlines, *zs))
    ys = moved(bylo, byhi, "gy", True)
    backs.append(own_backward(after(own, bylo), rw, cot, *BACKWARD_PARTS[1]))
    ys = after(ys, backs[1][0])
    bxlo, bxhi = call(back_x_kernel, "back_x", faces(4), (rest, rlines, *zs, *ys))
    xs = moved(bxlo, bxhi, "gx", True)
    backs.append(own_backward(after(own, bxlo), rw, cot, *BACKWARD_PARTS[2]))
    grad, force = call(
        partial(finish_kernel, len(backs)),
        "finish",
        [((CELLS, SLOTS, K), F32), ((2, 2, 3, 2, SLOTS), F32)],
        (counts, rest, rlines, *zs, *ys, *xs, *(b[0] for b in backs), *(b[1] for b in backs)),
        scalars=1,
    )
    return (
        new.reshape(2, 2, 2, SLOTS, K),
        jnp.transpose(force, (0, 1, 3, 2, 4)),
        grad.reshape(2, 2, 2, SLOTS, K),
    )


def solution(mesh):
    cells = P("gx", "gy", "gz", None, None)
    return jax.shard_map(
        shards,
        mesh=mesh,
        in_specs=(cells, cells, P("gx", "gy", "gz"), P("gx", "gy", "gz", None), P(), P(), P(), P()),
        out_specs=(cells, cells, cells),
        check_vma=False,
    )
```
